256 devices in a mesh: dp: 128 (over x_hi, y, z, core), sub: 2 (over x_lo).
Axes of the slice: x: 4 (x_hi: 2, x_lo: 2; x = x_hi * 2 + x_lo), y: 4, z: 8, core: 2. Of those that a mesh axis runs over, the one named last changes fastest.
Arguments:
- views: float32 [131072, 512], P(('dp', 'sub')), may hold values from -1 to 1
- log_sum_exp: float32 [131072], P(('dp', 'sub')), may hold values from 9.5 to 11.5
- loss_weight: float32 [131072], P(('dp', 'sub')), may hold values from 0.5 to 2
- partner: int32 [131072], P(('dp', 'sub')), may hold values from 0 to 131071, as said below
Outputs:
- grad_views: float32 [131072, 512], P(('dp', 'sub'))
The draws below stay inside these ranges and needn't reach their ends.
Inputs may be any that keep to these rules, and one draw needn't show every extreme that they name: partner is an involution without fixed points (partner[partner[i]] = i); the views of blocks 2k and 2k + 1, 1024 views each, are partners only among themselves.
All inputs are finite; a program needn't handle non-finite values.
Results may differ from the reference program's by a relative error of at most 0.0039.
Values may be sent and summed in bfloat16 or wider, within the bound.
No kernel may reach another device: no remote copies, remote signals or barrier semaphores. Data moves between devices by JAX's collectives and lax.ppermute only.
A program may use at most 128 MiB of HBM per device.

```python
import math
import jax
import jax.numpy as jnp
from jax import lax

D = 512
STEPS = 8
BLOCK = 1024
VIEWS = 131072
N_DP = 128


def draw_views(key, part):
    key = jax.random.fold_in(key, 11)
    key_cluster, key_center, key_noise = jax.random.split(key, 3)
    clusters = 4 * BLOCK
    member = jax.random.randint(key_cluster, (VIEWS,), 0, clusters)
    half_width = math.sqrt(3.0)
    centers = jax.random.uniform(key_center, (clusters, D), jnp.float32, -half_width, half_width)
    placed = centers[member]
    noise_part = jnp.clip(jax.random.normal(key_noise, (VIEWS, D), jnp.float32), -4.0, 4.0)
    mixed = 0.75 * placed + 0.6 * noise_part
    return (mixed * D ** (-0.5)).astype(jnp.float32)


def draw_partner(key, part):
    key = jax.random.fold_in(key, 29)
    pair_groups = VIEWS // (2 * BLOCK)
    group_keys = jax.random.split(key, pair_groups)
    orders = jax.vmap(lambda one_key: jax.random.permutation(one_key, 2 * BLOCK))(group_keys).astype(jnp.int32)
    starts = (jnp.arange(pair_groups, dtype=jnp.int32) * (2 * BLOCK))[:, None]
    lead_pos = (orders[:, 0::2] + starts).reshape(-1)
    follow_pos = (orders[:, 1::2] + starts).reshape(-1)
    final_output = jnp.zeros((VIEWS,), jnp.int32)
    final_output = final_output.at[lead_pos].set(follow_pos)
    final_output = final_output.at[follow_pos].set(lead_pos)
    return final_output


def block_levels(stream_key, shape, pieces, least, top_value):
    def one(axis_at, shards_of):
        heights = jax.random.uniform(jax.random.fold_in(jax.random.fold_in(stream_key, 6), axis_at), (shards_of,), jnp.float32, least / len(pieces), top_value / len(pieces))
        return jnp.repeat(jnp.exp(heights), shape[axis_at] // shards_of).reshape((-1,) + (1,) * (len(shape) - axis_at - 1))

    gain = one(*pieces[0])
    for cut in pieces[1:]:
        gain = gain * one(*cut)
    return gain


def setup_inputs(seed: int = 0) -> dict:
    streams_of = jax.random.split(jax.random.key(seed), 5)
    return {
        "views": draw_views(jax.random.fold_in(streams_of[4], 71), 0),
        "log_sum_exp": jnp.clip(9.5 + 2.0 * jax.random.uniform(streams_of[1], (VIEWS,), jnp.float32) ** block_levels(streams_of[1], (VIEWS,), ((0, 256),), -0.2, 0.2), 9.5, 11.5),
        "loss_weight": jnp.clip(jnp.exp(math.log(2.0) - 1.3862944 * jax.random.uniform(streams_of[2], (VIEWS,), jnp.float32) ** block_levels(streams_of[2], (VIEWS,), ((0, 256),), -0.2, 0.2)), 0.5, 2.0),
        "partner": draw_partner(jax.random.fold_in(streams_of[4], 71), 0),
    }


softmax_temper = 0.07


def reference(views, log_sum_exp, loss_weight, partner):
    views_bf = views.astype(jnp.bfloat16).reshape(N_DP, BLOCK, D)
    lse_blocks = log_sum_exp.reshape(N_DP, BLOCK)
    weight_blocks = loss_weight.reshape(N_DP, BLOCK)
    partner_blocks = partner.reshape(N_DP, BLOCK)
    within = jnp.arange(BLOCK, dtype=jnp.int32)

    def one_block(row_block):
        row_embeds = views_bf[row_block]
        row_index = row_block * BLOCK + within
        gradient_totals = jnp.zeros((BLOCK, D), jnp.float32)
        for offset in range(-(STEPS - 1), STEPS):
            col_block = (row_block + offset) % N_DP
            column_embeds = views_bf[col_block]
            col_index = col_block * BLOCK + within
            score_matrix = jnp.dot(row_embeds, column_embeds.T, preferred_element_type=jnp.float32) / softmax_temper
            paired_row = (partner_blocks[row_block][:, None] == col_index[None, :]).astype(jnp.float32)
            paired_col = (partner_blocks[col_block][None, :] == row_index[:, None]).astype(jnp.float32)
            pair_strength = weight_blocks[row_block][:, None] * (jnp.exp(score_matrix - lse_blocks[row_block][:, None]) - paired_row) + weight_blocks[col_block][None, :] * (jnp.exp(score_matrix - lse_blocks[col_block][None, :]) - paired_col)
            pair_strength = jnp.where(row_index[:, None] == col_index[None, :], jnp.float32(0.0), pair_strength)
            gradient_totals = gradient_totals + jnp.dot(pair_strength.astype(jnp.bfloat16), column_embeds, preferred_element_type=jnp.float32)
        return gradient_totals / softmax_temper

    grads = lax.map(one_block, jnp.arange(N_DP, dtype=jnp.int32))
    return grads.reshape(VIEWS, D)
```

```python
import functools
import math

import jax
import jax.numpy as jnp
from jax import lax
from jax.experimental import pallas as pl
from jax.experimental.pallas import tpu as pltpu
from jax.sharding import PartitionSpec as P

STEPS = 8
TEMPER = 0.07
SHIFT = 11.5
SCALE = math.log2(math.e) / TEMPER
OFFSET = SHIFT * math.log2(math.e)
EXTRA = 16
TILE = 256


def split3(value):
    high = value.astype(jnp.bfloat16)
    rest = value - high.astype(jnp.float32)
    mid = rest.astype(jnp.bfloat16)
    low = (rest - mid.astype(jnp.float32)).astype(jnp.bfloat16)
    return [high.astype(jnp.float32), mid.astype(jnp.float32), low.astype(jnp.float32)]


def pack_kernel(place_ref, views_ref, lse_ref, weight_ref, partner_ref, pack_ref):
    rows = views_ref.shape[0]
    pack_ref[:rows, :] = views_ref[...].astype(jnp.bfloat16)
    weight = weight_ref[...]
    strength = weight * jnp.exp(SHIFT - lse_ref[...])
    local = partner_ref[...] & 2047
    place = jnp.full(weight.shape, place_ref[0], jnp.int32).astype(jnp.float32)
    lines = split3(strength) + split3(weight)
    lines += [(local >> 8).astype(jnp.float32), (local & 255).astype(jnp.float32), place]
    lines += [jnp.zeros_like(weight)] * (EXTRA - len(lines))
    pack_ref[rows:, :] = jnp.concatenate(lines, axis=0).astype(jnp.bfloat16)


def pack_views(place, views, lse, weight, partner):
    rows, width = views.shape
    whole = pl.BlockSpec(memory_space=pltpu.VMEM)
    return pl.pallas_call(
        pack_kernel,
        out_shape=jax.ShapeDtypeStruct((rows + EXTRA, width), jnp.bfloat16),
        in_specs=[pl.BlockSpec(memory_space=pltpu.SMEM)] + [whole] * 4,
        out_specs=whole,
        name="pack",
    )(place, views, lse.reshape(1, rows), weight.reshape(1, rows), partner.reshape(1, rows))


def statistics(pack_ref):
    rows = pack_ref.shape[0] - EXTRA
    lines = pack_ref[rows:, :].astype(jnp.float32)
    strength = lines[0:1] + lines[1:2] + lines[2:3]
    weight = lines[3:4] + lines[4:5] + lines[5:6]
    partner = lines[6:7] * 256.0 + lines[7:8]
    place = lines[8:9] * float(rows)
    return strength, weight, partner, place


def spread(line):
    return jnp.broadcast_to(line, (128, line.shape[1])).T


def wide(column, width):
    return jnp.concatenate([column] * (width // 128), axis=1)


def scores_of(rows, cols):
    return lax.dot_general(rows, cols, (((1,), (1,)), ((), ())), preferred_element_type=jnp.float32)


def own_kernel(own_ref, other_ref, core_ref, rows_ref, strength_ref, total_ref):
    size = own_ref.shape[0] - EXTRA
    for half, row_pack in enumerate((other_ref, own_ref)):
        row_strength, row_weight, _, row_place = statistics(row_pack)
        row_strength, row_weight = spread(row_strength), spread(row_weight)
        strength_ref[half * size : (half + 1) * size, :] = row_strength
        rows_ref[half * size : (half + 1) * size, :] = row_pack[:size, :]
        for start in range(0, size, TILE):
            here = slice(start, start + TILE)
            rows = row_pack[here, :]
            total = None
            for which, col_pack in enumerate((own_ref, core_ref)):
                strength, weight, partner, _ = statistics(col_pack)
                cols = col_pack[:size, :]
                row_at = lax.broadcasted_iota(jnp.int32, (TILE, size), 0) + start
                raised = jnp.exp2(scores_of(rows, cols) * SCALE - OFFSET)
                value = raised * (wide(row_strength[here], size) + strength)
                pair = partner == row_at.astype(jnp.float32) + row_place
                value = value - jnp.where(pair, wide(row_weight[here], size) + weight, 0.0)
                if half == 1 and which == 0:
                    col_at = lax.broadcasted_iota(jnp.int32, (TILE, size), 1)
                    value = jnp.where(row_at == col_at, 0.0, value)
                term = jnp.dot(value.astype(jnp.bfloat16), cols, preferred_element_type=jnp.float32)
                total = term if total is None else total + term
            total_ref[half * size + start : half * size + start + TILE, :] = total


def own_terms(own, other, core):
    size, width = own.shape[0] - EXTRA, own.shape[1]
    whole = pl.BlockSpec(memory_space=pltpu.VMEM)
    return pl.pallas_call(
        own_kernel,
        out_shape=(
            jax.ShapeDtypeStruct((2 * size, width), jnp.bfloat16),
            jax.ShapeDtypeStruct((2 * size, 128), jnp.float32),
            jax.ShapeDtypeStruct((2 * size, width), jnp.float32),
        ),
        in_specs=[whole] * 3,
        out_specs=(whole,) * 3,
        compiler_params=pltpu.CompilerParams(vmem_limit_bytes=40 * 2**20),
        cost_estimate=pl.CostEstimate(flops=8 * size**2 * width, bytes_accessed=6 * 2**20, transcendentals=0),
        name="own",
    )(own, other, core)


def window_kernel(count, rows_ref, strength_ref, total_ref, *refs):
    col_packs, out_ref = refs[:count], refs[count]
    size = col_packs[0].shape[0] - EXTRA
    rows = rows_ref[...]
    row_strength = wide(strength_ref[...], size)
    total = total_ref[...]
    for col_pack in col_packs:
        lines = col_pack[size:, :].astype(jnp.float32)
        strength = lines[0:1] + lines[1:2] + lines[2:3]
        cols = col_pack[:size, :]
        raised = jnp.exp2(scores_of(rows, cols) * SCALE - OFFSET)
        value = (raised * (row_strength + strength)).astype(jnp.bfloat16)
        total = total + jnp.dot(value, cols, preferred_element_type=jnp.float32)
    out_ref[...] = total.astype(out_ref.dtype)


def window_terms(rows, strength, total, packs, first, tiles, dtype=jnp.float32):
    width = rows.shape[1]
    offset = 0 if total.shape[0] == tiles * TILE else first
    size = packs[0].shape[0] - EXTRA
    whole = pl.BlockSpec(packs[0].shape, lambda i: (0, 0))
    return pl.pallas_call(
        functools.partial(window_kernel, len(packs)),
        grid=(tiles,),
        out_shape=jax.ShapeDtypeStruct((tiles * TILE, width), dtype),
        in_specs=[
            pl.BlockSpec((TILE, width), lambda i: (i + first, 0)),
            pl.BlockSpec((TILE, 128), lambda i: (i + first, 0)),
            pl.BlockSpec((TILE, width), lambda i: (i + offset, 0)),
        ]
        + [whole] * len(packs),
        out_specs=pl.BlockSpec((TILE, width), lambda i: (i, 0)),
        compiler_params=pltpu.CompilerParams(vmem_limit_bytes=40 * 2**20),
        cost_estimate=pl.CostEstimate(
            flops=4 * len(packs) * tiles * TILE * size * width,
            bytes_accessed=tiles * TILE * width * 10 + len(packs) * size * width * 2,
            transcendentals=0,
        ),
        name="window",
    )(rows, strength, total, *packs)


def per_device(lines, views, log_sum_exp, loss_weight, partner):
    dp_place, sub_place = lax.axis_index("dp"), lax.axis_index("sub")
    loop_size = lax.axis_size("dp")
    chips = loop_size // 2

    onward = []
    for place in range(chips):
        turn = 1 if (place + 1) % (chips // lines) == 0 else 0
        later = (place + 1) % chips
        for sub in range(2):
            onward.append(((2 * place) * 2 + sub, (2 * later) * 2 + (sub ^ turn)))
            onward.append(((2 * later + 1) * 2 + (sub ^ turn), (2 * place + 1) * 2 + sub))
    cores = [(place, place ^ 1) for place in range(loop_size)]

    def chip_next(value):
        return lax.ppermute(value, ("dp", "sub"), onward)

    def core_swap(value):
        return lax.ppermute(value, "dp", cores)

    def sub_swap(value):
        return lax.ppermute(value, "sub", [(0, 1), (1, 0)])

    place = ((dp_place % 2) * 2 + sub_place).astype(jnp.int32).reshape(1)
    own = pack_views(place, views, log_sum_exp, loss_weight, partner)
    core = core_swap(own)
    same, cross = chip_next(own), chip_next(core)
    other = sub_swap(own)
    rows, strength, total = own_terms(own, other, core)
    tiles = rows.shape[0] // TILE
    reach = STEPS // 2
    for step in range(1, reach):
        next_same, next_cross = (chip_next(same) if step < reach - 1 else None), chip_next(cross)
        same_over, cross_over = core_swap(same), core_swap(cross)
        total = window_terms(rows, strength, total, (same, same_over), 0, tiles)
        total = window_terms(rows, strength, total, (cross, cross_over), 0, tiles)
        same, cross = next_same, next_cross
    away = sub_swap(window_terms(rows, strength, total, (cross,), 0, tiles // 2, jnp.bfloat16))
    here = window_terms(rows, strength, total, (cross,), tiles // 2, tiles // 2)
    return (here + away.astype(jnp.float32)) * (1.0 / TEMPER)


def solution(mesh):
    in_specs = (P(("dp", "sub"), None), P(("dp", "sub")), P(("dp", "sub")), P(("dp", "sub")))
    out_specs = P(("dp", "sub"), None)
    return jax.shard_map(
        functools.partial(per_device, 2), mesh=mesh, in_specs=in_specs, out_specs=out_specs, check_vma=False
    )
```

```python
import functools
import math

import jax
import jax.numpy as jnp
from jax import lax
from jax.experimental import pallas as pl
from jax.experimental.pallas import tpu as pltpu
from jax.sharding import PartitionSpec as P

STEPS = 8
TEMPER = 0.07
SHIFT = 11.5
SCALE = math.log2(math.e) / TEMPER
OFFSET = SHIFT * math.log2(math.e)
EXTRA = 16
VMEM = 24 * 2**20


def hold(value, token):
    return lax.optimization_barrier((value, token))[0]


def split3(value):
    high = value.astype(jnp.bfloat16)
    rest = value - high.astype(jnp.float32)
    mid = rest.astype(jnp.bfloat16)
    low = (rest - mid.astype(jnp.float32)).astype(jnp.bfloat16)
    return [high.astype(jnp.float32), mid.astype(jnp.float32), low.astype(jnp.float32)]


def pack_kernel(place_ref, views_ref, lse_ref, weight_ref, partner_ref, pack_ref):
    rows = views_ref.shape[0]
    pack_ref[:rows, :] = views_ref[...].astype(jnp.bfloat16)
    weight = weight_ref[...]
    strength = weight * jnp.exp(SHIFT - lse_ref[...])
    local = partner_ref[...] & 2047
    place = jnp.full(weight.shape, place_ref[0], jnp.int32).astype(jnp.float32)
    lines = split3(strength) + split3(weight)
    lines += [(local >> 8).astype(jnp.float32), (local & 255).astype(jnp.float32), place]
    lines += [jnp.zeros_like(weight)] * (EXTRA - len(lines))
    pack_ref[rows:, :] = jnp.concatenate(lines, axis=0).astype(jnp.bfloat16)


def pack_views(place, views, lse, weight, partner):
    rows, width = views.shape
    whole = pl.BlockSpec(memory_space=pltpu.VMEM)
    return pl.pallas_call(
        pack_kernel,
        out_shape=jax.ShapeDtypeStruct((rows + EXTRA, width), jnp.bfloat16),
        in_specs=[pl.BlockSpec(memory_space=pltpu.SMEM)] + [whole] * 4,
        out_specs=whole,
        name="pack",
    )(place, views, lse.reshape(1, rows), weight.reshape(1, rows), partner.reshape(1, rows))


def statistics(pack_ref):
    rows = pack_ref.shape[0] - EXTRA
    lines = pack_ref[rows:, :].astype(jnp.float32)
    strength = lines[0:1] + lines[1:2] + lines[2:3]
    weight = lines[3:4] + lines[4:5] + lines[5:6]
    partner = lines[6:7] * 256.0 + lines[7:8]
    place = lines[8:9] * float(rows)
    return strength, weight, partner, place


def spread(line):
    return jnp.broadcast_to(line, (128, line.shape[1])).T


def wide(column, width):
    return jnp.concatenate([column] * (width // 128), axis=1)


def scores_of(rows, cols):
    return lax.dot_general(rows, cols, (((1,), (1,)), ((), ())), preferred_element_type=jnp.float32)


def own_kernel(diagonal, row_pack, own_ref, core_ref, strength_ref, total_ref):
    size = own_ref.shape[0] - EXTRA
    row_strength, row_weight, _, row_place = statistics(row_pack)
    row_strength, row_weight = spread(row_strength), spread(row_weight)
    strength_ref[...] = row_strength
    rows = row_pack[:size, :]
    row_at = lax.broadcasted_iota(jnp.int32, (size, size), 0)
    total = None
    for which, col_pack in enumerate((own_ref, core_ref)):
        strength, weight, partner, _ = statistics(col_pack)
        cols = col_pack[:size, :]
        raised = jnp.exp2(scores_of(rows, cols) * SCALE - OFFSET)
        value = raised * (wide(row_strength, size) + strength)
        pair = partner == row_at.astype(jnp.float32) + row_place
        value = value - jnp.where(pair, wide(row_weight, size) + weight, 0.0)
        if diagonal and which == 0:
            col_at = lax.broadcasted_iota(jnp.int32, (size, size), 1)
            value = jnp.where(row_at == col_at, 0.0, value)
        term = jnp.dot(value.astype(jnp.bfloat16), cols, preferred_element_type=jnp.float32)
        total = term if total is None else total + term
    total_ref[...] = total


def own_terms(diagonal, rows, own, core):
    size, width = own.shape[0] - EXTRA, own.shape[1]
    whole = pl.BlockSpec(memory_space=pltpu.VMEM)
    return pl.pallas_call(
        functools.partial(own_kernel, diagonal),
        out_shape=(
            jax.ShapeDtypeStruct((size, 128), jnp.float32),
            jax.ShapeDtypeStruct((size, width), jnp.float32),
        ),
        in_specs=[whole] * 3,
        out_specs=(whole,) * 2,
        compiler_params=pltpu.CompilerParams(vmem_limit_bytes=VMEM),
        cost_estimate=pl.CostEstimate(flops=8 * size**2 * width, bytes_accessed=3 * 2**20, transcendentals=0),
        name="own_rows" if diagonal else "other_rows",
    )(rows, own, core)


def window_kernel(halves, count, *refs):
    row_packs, strengths, totals = refs[:halves], refs[halves : 2 * halves], refs[2 * halves : 3 * halves]
    col_packs, outs = refs[3 * halves : 3 * halves + count], refs[3 * halves + count :]
    size = col_packs[0].shape[0] - EXTRA
    for row_pack, row_strength, total_ref, out_ref in zip(row_packs, strengths, totals, outs, strict=True):
        total = total_ref[...]
        for col_pack in col_packs:
            lines = col_pack[size:, :].astype(jnp.float32)
            strength = lines[0:1] + lines[1:2] + lines[2:3]
            cols = col_pack[:size, :]
            raised = jnp.exp2(scores_of(row_pack[:size, :], cols) * SCALE - OFFSET)
            value = (raised * (wide(row_strength[...], size) + strength)).astype(jnp.bfloat16)
            total = total + jnp.dot(value, cols, preferred_element_type=jnp.float32)
        out_ref[...] = total.astype(out_ref.dtype)


def window_terms(row_packs, strengths, totals, col_packs, dtype=jnp.float32):
    halves, count = len(row_packs), len(col_packs)
    size, width = totals[0].shape
    whole = pl.BlockSpec(memory_space=pltpu.VMEM)
    return pl.pallas_call(
        functools.partial(window_kernel, halves, count),
        out_shape=(jax.ShapeDtypeStruct((size, width), dtype),) * halves,
        in_specs=[whole] * (3 * halves + count),
        out_specs=(whole,) * halves,
        input_output_aliases={2 * halves + i: i for i in range(halves)} if dtype == jnp.float32 else {},
        compiler_params=pltpu.CompilerParams(vmem_limit_bytes=VMEM),
        cost_estimate=pl.CostEstimate(
            flops=4 * count * halves * size**2 * width,
            bytes_accessed=halves * size * width * 10 + count * size * width * 2,
            transcendentals=0,
        ),
        name="window",
    )(*row_packs, *strengths, *totals, *col_packs)


def per_device(lines, views, log_sum_exp, loss_weight, partner):
    dp_place, sub_place = lax.axis_index("dp"), lax.axis_index("sub")
    loop_size = lax.axis_size("dp")
    chips = loop_size // 2

    onward = []
    for place in range(chips):
        turn = 1 if (place + 1) % (chips // lines) == 0 else 0
        later = (place + 1) % chips
        for sub in range(2):
            onward.append(((2 * place) * 2 + sub, (2 * later) * 2 + (sub ^ turn)))
            onward.append(((2 * later + 1) * 2 + (sub ^ turn), (2 * place + 1) * 2 + sub))
    cores = [(place, place ^ 1) for place in range(loop_size)]

    def chip_next(value):
        return lax.ppermute(value, ("dp", "sub"), onward)

    def core_swap(value):
        return lax.ppermute(value, "dp", cores)

    def sub_swap(value):
        return lax.ppermute(value, "sub", [(0, 1), (1, 0)])

    place = ((dp_place % 2) * 2 + sub_place).astype(jnp.int32).reshape(1)
    own = pack_views(place, views, log_sum_exp, loss_weight, partner)
    core = core_swap(own)
    same, cross = chip_next(own), chip_next(core)
    other = sub_swap(own)
    own_strength, own_total = own_terms(True, own, own, core)
    same = hold(same, own_total)
    other_strength, other_total = own_terms(False, other, own, core)
    cross = hold(cross, other_total)
    row_packs, strengths, totals = (other, own), (other_strength, own_strength), (other_total, own_total)
    reach = STEPS // 2
    for step in range(1, reach):
        next_same = chip_next(same) if step < reach - 1 else None
        same_over = core_swap(same)
        next_cross, cross_over = chip_next(cross), core_swap(cross)
        totals = window_terms(row_packs, strengths, totals, (same, same_over))
        next_same = hold(next_same, totals[0]) if step < reach - 1 else None
        totals = window_terms(row_packs, strengths, totals, (cross, cross_over))
        next_cross = hold(next_cross, totals[0])
        same, cross = next_same, next_cross
    away = sub_swap(window_terms(row_packs[:1], strengths[:1], totals[:1], (cross,), jnp.bfloat16)[0])
    here = window_terms(row_packs[1:], strengths[1:], totals[1:], (cross,))[0]
    return (here + away.astype(jnp.float32)) * (1.0 / TEMPER)


def solution(mesh):
    in_specs = (P(("dp", "sub"), None), P(("dp", "sub")), P(("dp", "sub")), P(("dp", "sub")))
    out_specs = P(("dp", "sub"), None)
    return jax.shard_map(
        functools.partial(per_device, 2), mesh=mesh, in_specs=in_specs, out_specs=out_specs, check_vma=False
    )
```

```python
import functools
import math

import jax
import jax.numpy as jnp
from jax import lax
from jax.experimental import pallas as pl
from jax.experimental.pallas import tpu as pltpu
from jax.sharding import PartitionSpec as P

STEPS = 8
TEMPER = 0.07
SHIFT = 11.5
SCALE = math.log2(math.e) / TEMPER
OFFSET = SHIFT * math.log2(math.e)
EXTRA = 16
VMEM = 16 * 2**20
CHUNKS = 2
ROWS_AT = 4
PLAN = {
    5: [(["core1"], "mine")],
    6: [(["own1"], "mine")],
    7: [(["core1"], "theirs")],
    8: [(["own1"], "theirs"), (["core2"], "theirs")],
    9: [(["own2"], "theirs")],
    10: [(["core2"], "mine"), (["own2"], "mine")],
    11: [(["core3"], "theirs")],
    12: [(["own3"], "theirs"), (["core3"], "mine")],
    13: [(["own3"], "mine")],
}
WHOLE = pl.BlockSpec(memory_space=pltpu.VMEM)


def hold(value, token):
    return lax.optimization_barrier((value, token))[0]


def split3(value):
    high = value.astype(jnp.bfloat16)
    rest = value - high.astype(jnp.float32)
    mid = rest.astype(jnp.bfloat16)
    low = (rest - mid.astype(jnp.float32)).astype(jnp.bfloat16)
    return [high.astype(jnp.float32), mid.astype(jnp.float32), low.astype(jnp.float32)]


def pack_kernel(place_ref, views_ref, lse_ref, weight_ref, partner_ref, whole_ref, *chunk_refs):
    total = views_ref.shape[0]
    rows = total // len(chunk_refs)
    weight = weight_ref[...]
    strength = weight * jnp.exp(SHIFT - lse_ref[...])
    local = partner_ref[...] & 2047
    place = jnp.full(weight.shape, place_ref[0] * total, jnp.int32).astype(jnp.float32)
    lines = split3(strength) + split3(weight)
    lines += [(local >> 8).astype(jnp.float32), (local & 255).astype(jnp.float32), place]
    lines += [jnp.zeros_like(weight)] * (EXTRA - len(lines))
    extra = jnp.concatenate(lines, axis=0).astype(jnp.bfloat16)
    chunk_refs[0][rows:, :] = extra
    whole_ref[total:, :] = extra
    for i, chunk_ref in enumerate(chunk_refs):
        chunk = views_ref[i * rows : (i + 1) * rows, :].astype(jnp.bfloat16)
        chunk_ref[:rows, :] = chunk
        whole_ref[i * rows : (i + 1) * rows, :] = chunk


def pack_views(place, views, lse, weight, partner):
    rows, width = views.shape
    shapes = [rows + EXTRA] + [rows // CHUNKS + (EXTRA if i == 0 else 0) for i in range(CHUNKS)]
    return pl.pallas_call(
        pack_kernel,
        out_shape=[jax.ShapeDtypeStruct((size, width), jnp.bfloat16) for size in shapes],
        in_specs=[pl.BlockSpec(memory_space=pltpu.SMEM)] + [WHOLE] * 4,
        out_specs=[WHOLE] * (CHUNKS + 1),
        compiler_params=pltpu.CompilerParams(vmem_limit_bytes=VMEM),
        name="pack",
    )(place, views, lse.reshape(1, rows), weight.reshape(1, rows), partner.reshape(1, rows))


def statistics(first_ref):
    rows = first_ref.shape[0] - EXTRA
    lines = first_ref[rows:, :].astype(jnp.float32)
    strength = lines[0:1] + lines[1:2] + lines[2:3]
    weight = lines[3:4] + lines[4:5] + lines[5:6]
    partner = lines[6:7] * 256.0 + lines[7:8]
    return strength, weight, partner, lines[8:9]


def joined(chunk_refs):
    first = chunk_refs[0][: chunk_refs[0].shape[0] - EXTRA, :]
    rest = [ref[...] for ref in chunk_refs[1:]]
    return jnp.concatenate([first] + rest, axis=0) if rest else first


def spread(line):
    return jnp.broadcast_to(line, (128, line.shape[1])).T


def wide(column, width):
    return jnp.concatenate([column] * (width // 128), axis=1)


def scores_of(rows, cols):
    return lax.dot_general(rows, cols, (((1,), (1,)), ((), ())), preferred_element_type=jnp.float32)


def own_kernel(diagonal, row_ref, own_ref, *refs):
    row_refs, own_refs, core_refs = [row_ref], [own_ref], refs[:CHUNKS]
    strength_ref, total_ref = refs[CHUNKS:]
    size = total_ref.shape[0]
    row_strength, row_weight, _, row_place = statistics(row_refs[0])
    row_strength, row_weight = spread(row_strength), spread(row_weight)
    strength_ref[...] = row_strength
    rows = joined(row_refs)
    row_at = lax.broadcasted_iota(jnp.int32, (size, size), 0)
    total = None
    for which, col_refs in enumerate((own_refs, core_refs)):
        strength, weight, partner, _ = statistics(col_refs[0])
        cols = joined(col_refs)
        raised = jnp.exp2(scores_of(rows, cols) * SCALE - OFFSET)
        value = raised * (wide(row_strength, size) + strength)
        pair = partner == row_at.astype(jnp.float32) + row_place
        value = value - jnp.where(pair, wide(row_weight, size) + weight, 0.0)
        if diagonal and which == 0:
            col_at = lax.broadcasted_iota(jnp.int32, (size, size), 1)
            value = jnp.where(row_at == col_at, 0.0, value)
        term = jnp.dot(value.astype(jnp.bfloat16), cols, preferred_element_type=jnp.float32)
        total = term if total is None else total + term
    total_ref[...] = total


def own_terms(diagonal, rows, own, core):
    size, width = own.shape[0] - EXTRA, own.shape[1]
    return pl.pallas_call(
        functools.partial(own_kernel, diagonal),
        out_shape=(
            jax.ShapeDtypeStruct((size, 128), jnp.float32),
            jax.ShapeDtypeStruct((size, width), jnp.float32),
        ),
        in_specs=[WHOLE] * (2 + CHUNKS),
        out_specs=(WHOLE,) * 2,
        compiler_params=pltpu.CompilerParams(vmem_limit_bytes=VMEM),
        cost_estimate=pl.CostEstimate(flops=8 * size**2 * width, bytes_accessed=3 * 2**20, transcendentals=0),
        name="own_rows" if diagonal else "other_rows",
    )(rows, own, *core)


def spread_kernel(*refs):
    count = len(refs) // 2
    for first_ref, out_ref in zip(refs[:count], refs[count:], strict=True):
        out_ref[...] = spread(statistics(first_ref)[0])


def spread_strengths(packs):
    size = packs[1][0].shape[0] - EXTRA
    return pl.pallas_call(
        spread_kernel,
        out_shape=(jax.ShapeDtypeStruct((size, 128), jnp.float32),) * len(packs),
        in_specs=[WHOLE] * len(packs),
        out_specs=(WHOLE,) * len(packs),
        compiler_params=pltpu.CompilerParams(vmem_limit_bytes=VMEM),
        name="spread",
    )(*[pack[0] for pack in packs])


def window_kernel(row_counts, strides, count, *refs):
    refs = list(refs)
    row_packs = [[refs.pop(0) for _ in range(chunks)] for chunks in row_counts]
    strengths = [refs.pop(0) for _ in row_counts]
    totals = [refs.pop(0) for _ in strides]
    col_packs = [[refs.pop(0) for _ in range(CHUNKS)] for _ in range(count)]
    size = strengths[0].shape[0]
    for at, (row_pack, row_strength) in enumerate(zip(row_packs, strengths, strict=True)):
        total, pieces = None, {}
        for col_refs in col_packs:
            strength, _, _, _ = statistics(col_refs[0])
            cols = joined(col_refs)
            raised = jnp.exp2(scores_of(joined(row_pack), cols) * SCALE - OFFSET)
            value = (raised * (wide(row_strength[...], size) + strength)).astype(jnp.bfloat16)
            term = jnp.dot(value, cols, preferred_element_type=jnp.float32)
            total = term if total is None else total + term
        for total_ref, (row, begin, offset) in zip(totals, strides, strict=True):
            if row == at and total_ref.shape[0] >= size:
                total = total + total_ref[offset : offset + size, :]
            elif row == at:
                pieces.setdefault(begin, []).append(total_ref[...].astype(jnp.float32))
        if pieces:
            total = total + jnp.concatenate([pieces[begin][0] for begin in sorted(pieces)], axis=0)
        first = 0
        for out_ref in refs:
            begin, end = max(first, at * size), min(first + out_ref.shape[0], (at + 1) * size)
            if begin < end:
                piece = total[begin - at * size : end - at * size, :]
                out_ref[begin - first : end - first, :] = piece.astype(out_ref.dtype)
            first += out_ref.shape[0]


def window_terms(row_packs, strengths, totals, col_packs, dtype=jnp.float32, alias=False, pieces=1):
    size, width = strengths[0].shape[0], col_packs[0][0].shape[1]
    strides = []
    arrays = []
    for row, array, offset in totals:
        for i, piece in enumerate(array if offset is None else [array]):
            strides.append((row, i * piece.shape[0] if offset is None else 0, offset or 0))
            arrays.append(piece)
    at = sum(len(pack) for pack in row_packs) + len(row_packs)
    return pl.pallas_call(
        functools.partial(window_kernel, tuple(len(pack) for pack in row_packs), tuple(strides), len(col_packs)),
        out_shape=[jax.ShapeDtypeStruct((len(row_packs) * size // pieces, width), dtype)] * pieces,
        in_specs=[WHOLE] * (at + len(arrays) + CHUNKS * len(col_packs)),
        out_specs=[WHOLE] * pieces,
        input_output_aliases={at: 0} if alias else {},
        compiler_params=pltpu.CompilerParams(vmem_limit_bytes=VMEM),
        cost_estimate=pl.CostEstimate(
            flops=4 * len(row_packs) * len(col_packs) * size**2 * width,
            bytes_accessed=len(row_packs) * size * width * 10,
            transcendentals=0,
        ),
        name="window",
    )(*sum(row_packs, []), *strengths, *arrays, *sum(col_packs, []))


def finish_kernel(here_ref, *refs):
    rows = here_ref.shape[0]
    away_ref, out_ref = refs[-2:]
    count = len(refs) - 2
    for i, piece_ref in enumerate(refs[:count]):
        part = slice(i * rows // count, (i + 1) * rows // count)
        total = here_ref[part, :] + piece_ref[...].astype(jnp.float32) + away_ref[part, :].astype(jnp.float32)
        out_ref[part, :] = total * (1.0 / TEMPER)


def finish(here, pieces, away):
    return pl.pallas_call(
        finish_kernel,
        out_shape=jax.ShapeDtypeStruct(here.shape, jnp.float32),
        in_specs=[WHOLE] * (2 + len(pieces)),
        out_specs=WHOLE,
        compiler_params=pltpu.CompilerParams(vmem_limit_bytes=VMEM),
        name="finish",
    )(here, *pieces, away)


def per_device(lines, views, log_sum_exp, loss_weight, partner):
    dp_place, sub_place = lax.axis_index("dp"), lax.axis_index("sub")
    loop_size = lax.axis_size("dp")
    chips = loop_size // 2

    onward = []
    for place in range(chips):
        turn = 1 if (place + 1) % (chips // lines) == 0 else 0
        later = (place + 1) % chips
        for sub in range(2):
            onward.append(((2 * place) * 2 + sub, (2 * later) * 2 + (sub ^ turn)))
            onward.append(((2 * later + 1) * 2 + (sub ^ turn), (2 * place + 1) * 2 + sub))
    cores = [(place, place ^ 1) for place in range(loop_size)]

    def chip_next(value):
        return lax.ppermute(value, ("dp", "sub"), onward)

    def core_swap(value):
        return lax.ppermute(value, "dp", cores)

    def sub_swap(value):
        return lax.ppermute(value, "sub", [(0, 1), (1, 0)])

    def every(move, pack):
        return [move(chunk) for chunk in pack]

    place = ((dp_place % 2) * 2 + sub_place).astype(jnp.int32).reshape(1)
    whole, *own = pack_views(place, views, log_sum_exp, loss_weight, partner)
    core = every(core_swap, own)
    coming = {"core": every(chip_next, core), "own": every(chip_next, own)}
    other = sub_swap(whole)
    size = views.shape[0]
    own_strength, own_total = own_terms(True, whole, whole, core)
    token = own_total

    reach = STEPS // 2
    legs = [(kind, step) for step in range(1, reach) for kind in ("core", "own")] + [("core", reach)]
    plan = PLAN
    packs, strengths, totals, columns = {}, {}, {}, {}
    arrivals, back = 0, None
    for kind, step in legs:
        arrived, sent = [], []
        columns[f"{kind}{step}"] = arrived
        for chunk in coming[kind]:
            chunk = hold(chunk, token)
            arrived.append(chunk)
            if step < reach - (kind == "own"):
                sent.append(chip_next(chunk))
            arrivals += 1
            if arrivals == ROWS_AT:
                other = hold(other, chunk)
                other_strength, other_total = own_terms(False, other, whole, core)
                far = core_swap(other)
                packs = {"mine": [[whole], [other]], "theirs": [core, [far]]}
                strengths["mine"] = [own_strength, other_strength]
                totals["mine"] = [(0, own_total, 0), (1, other_total, 0)]
                token = other_total
            for names, rows in plan.get(arrivals, ()):
                cols = [columns[name] for name in names]
                if rows == "theirs" and rows not in strengths:
                    strengths[rows] = spread_strengths((core, [far]))
                parts = [(row, hold(hold(array, chunk), token), offset) for row, array, offset in totals.get(rows, [])]
                alias = len(parts) > 0 and parts[0][1].shape[0] == 2 * size
                if alias:
                    parts = [(row, parts[0][1], offset) for row, _, offset in parts]
                if rows == "theirs" and names[-1] == f"own{reach - 1}":
                    everything = parts[0][1]
                    back = window_terms(
                        packs[rows][1:], strengths[rows][1:], [(0, everything, size)], cols, jnp.bfloat16, pieces=2
                    )
                    token = window_terms(
                        packs[rows][:1], strengths[rows][:1], [(0, hold(everything, back[0]), 0)], cols, jnp.bfloat16, pieces=2
                    )
                    back, back_own = every(core_swap, back), every(core_swap, token)
                    token = token[0]
                    continue
                (token,) = window_terms(packs[rows], strengths[rows], parts, cols, alias=alias)
                totals[rows] = [(0, token, 0), (1, token, size)]
        coming[kind] = sent
    mine = totals["mine"][0][1]
    (away,) = window_terms(
        packs["mine"][1:], strengths["mine"][1:], [(0, mine, size), (0, back, None)], [arrived], jnp.bfloat16
    )
    away = sub_swap(away)
    (here,) = window_terms(packs["mine"][:1], strengths["mine"][:1], [(0, mine, 0)], [arrived])
    here = finish(here, back_own, away)
    return here


def solution(mesh):
    in_specs = (P(("dp", "sub"), None), P(("dp", "sub")), P(("dp", "sub")), P(("dp", "sub")))
    out_specs = P(("dp", "sub"), None)
    return jax.shard_map(
        functools.partial(per_device, 2), mesh=mesh, in_specs=in_specs, out_specs=out_specs, check_vma=False
    )
```

```python
import functools
import math

import jax
import jax.numpy as jnp
from jax import lax
from jax.experimental import pallas as pl
from jax.experimental.pallas import tpu as pltpu
from jax.sharding import PartitionSpec as P

STEPS = 8
TEMPER = 0.07
SHIFT = 11.5
SCALE = math.log2(math.e) / TEMPER
OFFSET = SHIFT * math.log2(math.e)
EXTRA = 16
CHUNKS = 1
GROUPS = 2
VMEM = 8 * 2**20
WHOLE = pl.BlockSpec(memory_space=pltpu.VMEM)

PLAN = {
    1: [("core1", ("own", "core"))],
    2: [("own1", ("own", "core"))],
    3: [("core2", ("own", "core"))],
    4: [("core1", ("other", "far")), ("own1", ("other", "far")), ("core2", ("other", "far"))],
    5: [("own2", ("own", "core")), ("own2", ("other", "far")), ("core3", ("core", "far")), ("core3", ("own", "other"))],
    6: [("own3", ("far",)), ("own3", ("core",)), ("own3", ("own", "other"))],
}
ROWS_AT = 3


def hold(value, token):
    return lax.optimization_barrier((value, token))[0]


def call(kernel, shapes, args, name, aliases=None, flops=0, specs=None):
    return pl.pallas_call(
        kernel,
        out_shape=[jax.ShapeDtypeStruct(shape, dtype) for shape, dtype in shapes],
        in_specs=specs or [WHOLE] * len(args),
        out_specs=[WHOLE] * len(shapes),
        input_output_aliases=aliases or {},
        compiler_params=pltpu.CompilerParams(vmem_limit_bytes=VMEM),
        cost_estimate=pl.CostEstimate(flops=flops, bytes_accessed=0, transcendentals=0),
        name=name,
    )(*args)


def split3(value):
    high = value.astype(jnp.bfloat16)
    rest = value - high.astype(jnp.float32)
    mid = rest.astype(jnp.bfloat16)
    low = (rest - mid.astype(jnp.float32)).astype(jnp.bfloat16)
    return [high.astype(jnp.float32), mid.astype(jnp.float32), low.astype(jnp.float32)]


def pack_kernel(place_ref, views_ref, lse_ref, weight_ref, partner_ref, pack_ref):
    rows = views_ref.shape[0]
    pack_ref[:rows, :] = views_ref[...].astype(jnp.bfloat16)
    weight = weight_ref[...]
    strength = weight * jnp.exp(SHIFT - lse_ref[...])
    local = partner_ref[...] & 2047
    place = jnp.full(weight.shape, place_ref[0] * rows, jnp.int32).astype(jnp.float32)
    lines = split3(strength) + split3(weight)
    lines += [(local >> 8).astype(jnp.float32), (local & 255).astype(jnp.float32), place]
    lines += [jnp.zeros_like(weight)] * (EXTRA - len(lines))
    pack_ref[rows:, :] = jnp.concatenate(lines, axis=0).astype(jnp.bfloat16)


def pack_views(place, views, lse, weight, partner):
    rows, width = views.shape
    line = (1, rows)
    return call(
        pack_kernel,
        [((rows + EXTRA, width), jnp.bfloat16)],
        (place, views, lse.reshape(line), weight.reshape(line), partner.reshape(line)),
        "pack",
        specs=[pl.BlockSpec(memory_space=pltpu.SMEM)] + [WHOLE] * 4,
    )[0]


def statistics(first_ref):
    rows = first_ref.shape[0] - EXTRA
    lines = first_ref[rows:, :].astype(jnp.float32)
    strength = lines[0:1] + lines[1:2] + lines[2:3]
    weight = lines[3:4] + lines[4:5] + lines[5:6]
    partner = lines[6:7] * 256.0 + lines[7:8]
    return strength, weight, partner, lines[8:9]


def joined(chunk_refs):
    first = chunk_refs[0][: chunk_refs[0].shape[0] - EXTRA, :]
    rest = [ref[...] for ref in chunk_refs[1:]]
    return jnp.concatenate([first] + rest, axis=0) if rest else first


def spread(line):
    return jnp.broadcast_to(line, (128, line.shape[1])).T


def wide(column, width):
    return jnp.concatenate([column] * (width // 128), axis=1)


def scores_of(rows, cols):
    return lax.dot_general(rows, cols, (((1,), (1,)), ((), ())), preferred_element_type=jnp.float32)


def block_kernel(diagonal, row_ref, own_ref, *refs):
    core_refs, (strength_ref, total_ref) = refs[:CHUNKS], refs[CHUNKS:]
    size = total_ref.shape[0]
    row_strength, row_weight, _, row_place = statistics(row_ref)
    row_strength, row_weight = spread(row_strength), spread(row_weight)
    strength_ref[...] = row_strength
    rows = joined([row_ref])
    row_at = lax.broadcasted_iota(jnp.int32, (size, size), 0)
    total = None
    for col_refs in ([own_ref], core_refs):
        strength, weight, partner, _ = statistics(col_refs[0])
        cols = joined(col_refs)
        raised = jnp.exp2(scores_of(rows, cols) * SCALE - OFFSET)
        value = raised * (wide(row_strength, size) + strength)
        pair = partner == row_at.astype(jnp.float32) + row_place
        value = value - jnp.where(pair, wide(row_weight, size) + weight, 0.0)
        if diagonal and total is None:
            col_at = lax.broadcasted_iota(jnp.int32, (size, size), 1)
            value = jnp.where(row_at == col_at, 0.0, value)
        term = jnp.dot(value.astype(jnp.bfloat16), cols, preferred_element_type=jnp.float32)
        total = term if total is None else total + term
    total_ref[...] = total


def block_terms(diagonal, rows, own, core):
    size, width = own.shape[0] - EXTRA, own.shape[1]
    return call(
        functools.partial(block_kernel, diagonal),
        [((size, 128), jnp.float32), ((size, width), jnp.float32)],
        (rows, own, *core),
        "own_rows" if diagonal else "other_rows",
        flops=32 * size**2 * width,
    )


def spread_kernel(first_ref, out_ref):
    out_ref[...] = spread(statistics(first_ref)[0])


def strengths_of(pack, size):
    return call(spread_kernel, [((size, 128), jnp.float32)], pack[:1], "spread")[0]


def window_kernel(layout, pieces, *refs):
    refs = list(refs)
    parts = []
    for chunks, addends in layout:
        pack, strength = [refs.pop(0) for _ in range(chunks)], refs.pop(0)
        parts.append((pack, strength, [[refs.pop(0) for _ in range(count)] for count in addends]))
    cols_refs = [refs.pop(0) for _ in range(CHUNKS)]
    strength, _, _, _ = statistics(cols_refs[0])
    cols = joined(cols_refs)
    for at, (pack, row_strength, addends) in enumerate(parts):
        size = row_strength.shape[0]
        raised = jnp.exp2(scores_of(joined(pack), cols) * SCALE - OFFSET)
        value = (raised * (wide(row_strength[...], size) + strength)).astype(jnp.bfloat16)
        total = jnp.dot(value, cols, preferred_element_type=jnp.float32)
        for addend in addends:
            whole = [ref[...].astype(jnp.float32) for ref in addend]
            total = total + (jnp.concatenate(whole, axis=0) if len(whole) > 1 else whole[0])
        for i, out_ref in enumerate(refs[at * pieces : (at + 1) * pieces]):
            rows = out_ref.shape[0]
            out_ref[...] = total[i * rows : (i + 1) * rows, :].astype(out_ref.dtype)


def window_terms(row_packs, cols, dtype=jnp.float32, pieces=1, weight=0):
    size, width = row_packs[0][1].shape[0], cols[0].shape[1]
    args, layout, aliases = [], [], {}
    for at, (pack, strength, addends) in enumerate(row_packs):
        layout.append((len(pack), tuple(len(addend) for addend in addends)))
        args += [*pack, strength]
        if addends and len(addends[0]) == pieces and dtype == addends[0][0].dtype:
            aliases.update({len(args) + i: at * pieces + i for i in range(pieces)})
        args += sum(addends, [])
    return call(
        functools.partial(window_kernel, tuple(layout), pieces),
        [((size // pieces, width), dtype)] * (pieces * len(row_packs)),
        (*args, *cols),
        "window",
        aliases=aliases,
        flops=weight * len(row_packs) * size**2 * width,
    )


def finish_kernel(here_ref, *refs):
    pieces, (away_ref, out_ref) = refs[:-2], refs[-2:]
    rows = here_ref.shape[0] // len(pieces)
    for i, piece_ref in enumerate(pieces):
        part = slice(i * rows, (i + 1) * rows)
        total = here_ref[part, :] + piece_ref[...].astype(jnp.float32) + away_ref[part, :].astype(jnp.float32)
        out_ref[part, :] = total * (1.0 / TEMPER)


def per_device(views, log_sum_exp, loss_weight, partner):
    dp_place, sub_place = lax.axis_index("dp"), lax.axis_index("sub")
    loop_size = lax.axis_size("dp")
    chips = loop_size // 2
    size = views.shape[0]

    onward = []
    for place in range(chips):
        turn = 1 if (place + 1) % (chips // GROUPS) == 0 else 0
        later = (place + 1) % chips
        for sub in range(2):
            onward.append(((2 * place) * 2 + sub, (2 * later) * 2 + (sub ^ turn)))
            onward.append(((2 * later + 1) * 2 + (sub ^ turn), (2 * place + 1) * 2 + sub))
    cores = [(place, place ^ 1) for place in range(loop_size)]

    def chip_next(value):
        return lax.ppermute(value, ("dp", "sub"), onward)

    def core_swap(value):
        return lax.ppermute(value, "dp", cores)

    def sub_swap(value):
        return lax.ppermute(value, "sub", [(0, 1), (1, 0)])

    place = ((dp_place % 2) * 2 + sub_place).astype(jnp.int32).reshape(1)
    whole = pack_views(place, views, log_sum_exp, loss_weight, partner)
    core = core_swap(whole)
    coming = {"core": chip_next(core), "own": chip_next(hold(whole, core))}
    other = sub_swap(whole)

    reach = STEPS // 2
    legs = [(kind, step) for step in range(1, reach) for kind in ("core", "own")] + [("core", reach)]
    packs = {"own": [whole], "core": [core]}
    strengths, totals, columns = {}, {"core": [], "far": []}, {}
    strengths["own"], token = block_terms(True, whole, whole, [core])
    totals["own"] = [[token]]
    strengths["core"] = strengths_of([core], size)
    for arrivals, (kind, step) in enumerate(legs, 1):
        pack = hold(coming[kind], token)
        arrived = columns[f"{kind}{step}"] = [pack]
        if step < reach - (kind == "own"):
            coming[kind] = chip_next(pack)
        for name, rows in PLAN.get(arrivals, ()):
            group = [
                (packs[r], strengths[r], [[hold(hold(a, pack), token) for a in addend] for addend in totals[r]])
                for r in rows
            ]
            last = name == f"own{reach - 1}" and rows[0] in ("core", "far")
            if last:
                sums = window_terms(group, columns[name], jnp.bfloat16)
                totals[rows[0]] = [sums]
            else:
                sums = window_terms(group, columns[name], weight=16 if arrivals < 3 else 0)
                totals.update({r: [[value]] for r, value in zip(rows, sums, strict=True)})
            token = sums[0]
        if arrivals == ROWS_AT:
            other = hold(hold(other, pack), token)
            strengths["other"], token = block_terms(False, other, whole, [core])
            far = core_swap(other)
            packs["other"], packs["far"] = [other], [far]
            totals["other"] = [[token]]
            strengths["far"] = strengths_of([far], size)
    back = {r: [core_swap(piece) for piece in totals[r][0]] for r in ("far", "core")}
    (away,) = window_terms([(packs["other"], strengths["other"], totals["other"] + [back["far"]])], arrived, jnp.bfloat16)
    away = sub_swap(away)
    (here,) = window_terms([(packs["own"], strengths["own"], totals["own"])], arrived)
    return call(finish_kernel, [(here.shape, jnp.float32)], (here, *back["core"], away), "finish")[0]


def solution(mesh):
    in_specs = (P(("dp", "sub"), None), P(("dp", "sub")), P(("dp", "sub")), P(("dp", "sub")))
    out_specs = P(("dp", "sub"), None)
    return jax.shard_map(per_device, mesh=mesh, in_specs=in_specs, out_specs=out_specs, check_vma=False)
```

```python
import functools
import math

import jax
import jax.numpy as jnp
from jax import lax
from jax.experimental import pallas as pl
from jax.experimental.pallas import tpu as pltpu
from jax.sharding import PartitionSpec as P

STEPS = 8
TEMPER = 0.07
SHIFT = 11.5
SCALE = math.log2(math.e) / TEMPER
OFFSET = SHIFT * math.log2(math.e)
EXTRA = 16
CHUNKS = 2
GROUPS = 2
VMEM = 8 * 2**20
WHOLE = pl.BlockSpec(memory_space=pltpu.VMEM)

PLAN = {
    2: [("core1", ("own", "core"))],
    3: [("own1", ("own", "core"))],
    6: [("core1", ("other", "far"))],
    7: [("own1", ("other", "far"))],
    8: [("core2", ("other", "far")), ("own2", ("other", "far")), ("core3", ("other", "far"))],
    9: [("own3", ("far",)), ("own3", ("other",))],
}
BESIDE = [(name, ("own", "core")) for name in ("core2", "own2", "core3")] + [("own3", ("core",)), ("own3", ("own",))]
ROWS_AT = 5


def hold(value, token):
    return lax.optimization_barrier((value, token))[0]


def call(kernel, shapes, args, name, aliases=None, flops=0, specs=None):
    return pl.pallas_call(
        kernel,
        out_shape=[jax.ShapeDtypeStruct(shape, dtype) for shape, dtype in shapes],
        in_specs=specs or [WHOLE] * len(args),
        out_specs=[WHOLE] * len(shapes),
        input_output_aliases=aliases or {},
        compiler_params=pltpu.CompilerParams(vmem_limit_bytes=VMEM),
        cost_estimate=pl.CostEstimate(flops=flops, bytes_accessed=0, transcendentals=0),
        name=name,
    )(*args)


def split3(value):
    high = value.astype(jnp.bfloat16)
    rest = value - high.astype(jnp.float32)
    mid = rest.astype(jnp.bfloat16)
    low = (rest - mid.astype(jnp.float32)).astype(jnp.bfloat16)
    return [high.astype(jnp.float32), mid.astype(jnp.float32), low.astype(jnp.float32)]


def pack_kernel(place_ref, views_ref, lse_ref, weight_ref, partner_ref, whole_ref, *chunk_refs):
    total = views_ref.shape[0]
    rows = total // CHUNKS
    weight = weight_ref[...]
    strength = weight * jnp.exp(SHIFT - lse_ref[...])
    local = partner_ref[...] & 2047
    place = jnp.full(weight.shape, place_ref[0] * total, jnp.int32).astype(jnp.float32)
    lines = split3(strength) + split3(weight)
    lines += [(local >> 8).astype(jnp.float32), (local & 255).astype(jnp.float32), place]
    lines += [jnp.zeros_like(weight)] * (EXTRA - len(lines))
    extra = jnp.concatenate(lines, axis=0).astype(jnp.bfloat16)
    chunk_refs[0][rows:, :] = extra
    whole_ref[total:, :] = extra
    for i, chunk_ref in enumerate(chunk_refs):
        chunk = views_ref[i * rows : (i + 1) * rows, :].astype(jnp.bfloat16)
        chunk_ref[:rows, :] = chunk
        whole_ref[i * rows : (i + 1) * rows, :] = chunk


def pack_views(place, views, lse, weight, partner):
    rows, width = views.shape
    sizes = [rows + EXTRA] + [rows // CHUNKS + (EXTRA if i == 0 else 0) for i in range(CHUNKS)]
    line = (1, rows)
    return call(
        pack_kernel,
        [((size, width), jnp.bfloat16) for size in sizes],
        (place, views, lse.reshape(line), weight.reshape(line), partner.reshape(line)),
        "pack",
        specs=[pl.BlockSpec(memory_space=pltpu.SMEM)] + [WHOLE] * 4,
    )


def statistics(first_ref):
    rows = first_ref.shape[0] - EXTRA
    lines = first_ref[rows:, :].astype(jnp.float32)
    strength = lines[0:1] + lines[1:2] + lines[2:3]
    weight = lines[3:4] + lines[4:5] + lines[5:6]
    partner = lines[6:7] * 256.0 + lines[7:8]
    return strength, weight, partner, lines[8:9]


def joined(chunk_refs):
    first = chunk_refs[0][: chunk_refs[0].shape[0] - EXTRA, :]
    rest = [ref[...] for ref in chunk_refs[1:]]
    return jnp.concatenate([first] + rest, axis=0) if rest else first


def spread(line):
    return jnp.broadcast_to(line, (128, line.shape[1])).T


def wide(column, width):
    return jnp.concatenate([column] * (width // 128), axis=1)


def scores_of(rows, cols):
    return lax.dot_general(rows, cols, (((1,), (1,)), ((), ())), preferred_element_type=jnp.float32)


def block_kernel(count, diagonal, *refs):
    row_refs, own_ref, refs = refs[:count], refs[count], refs[count + 1 :]
    core_refs, (strength_ref, total_ref) = refs[:CHUNKS], refs[CHUNKS:]
    size = total_ref.shape[0]
    row_strength, row_weight, _, row_place = statistics(row_refs[0])
    row_strength, row_weight = spread(row_strength), spread(row_weight)
    strength_ref[...] = row_strength
    rows = joined(row_refs)
    row_at = lax.broadcasted_iota(jnp.int32, (size, size), 0)
    total = None
    for col_refs in ([own_ref], core_refs):
        strength, weight, partner, _ = statistics(col_refs[0])
        cols = joined(col_refs)
        raised = jnp.exp2(scores_of(rows, cols) * SCALE - OFFSET)
        value = raised * (wide(row_strength, size) + strength)
        pair = partner == row_at.astype(jnp.float32) + row_place
        value = value - jnp.where(pair, wide(row_weight, size) + weight, 0.0)
        if diagonal and total is None:
            col_at = lax.broadcasted_iota(jnp.int32, (size, size), 1)
            value = jnp.where(row_at == col_at, 0.0, value)
        term = jnp.dot(value.astype(jnp.bfloat16), cols, preferred_element_type=jnp.float32)
        total = term if total is None else total + term
    total_ref[...] = total


def block_terms(diagonal, rows, own, core):
    size, width = own.shape[0] - EXTRA, own.shape[1]
    return call(
        functools.partial(block_kernel, len(rows), diagonal),
        [((size, 128), jnp.float32), ((size, width), jnp.float32)],
        (*rows, own, *core),
        "own_rows" if diagonal else "other_rows",
        flops=32 * size**2 * width,
    )


def spread_kernel(first_ref, out_ref):
    out_ref[...] = spread(statistics(first_ref)[0])


def strengths_of(pack, size):
    return call(spread_kernel, [((size, 128), jnp.float32)], pack[:1], "spread")[0]


def window_kernel(layout, pieces, count, *refs):
    refs = list(refs)
    parts = []
    for chunks, addends in layout:
        pack, strength = [refs.pop(0) for _ in range(chunks)], refs.pop(0)
        parts.append((pack, strength, [[refs.pop(0) for _ in range(count)] for count in addends]))
    cols_refs = [refs.pop(0) for _ in range(count)]
    strength, _, _, _ = statistics(cols_refs[0])
    cols = joined(cols_refs)
    for at, (pack, row_strength, addends) in enumerate(parts):
        size = row_strength.shape[0]
        raised = jnp.exp2(scores_of(joined(pack), cols) * SCALE - OFFSET)
        value = (raised * (wide(row_strength[...], size) + strength)).astype(jnp.bfloat16)
        total = jnp.dot(value, cols, preferred_element_type=jnp.float32)
        for addend in addends:
            whole = [ref[...].astype(jnp.float32) for ref in addend]
            total = total + (jnp.concatenate(whole, axis=0) if len(whole) > 1 else whole[0])
        for i, out_ref in enumerate(refs[at * pieces : (at + 1) * pieces]):
            rows = out_ref.shape[0]
            out_ref[...] = total[i * rows : (i + 1) * rows, :].astype(out_ref.dtype)


def window_terms(row_packs, cols, dtype=jnp.float32, pieces=1, weight=0):
    size, width = row_packs[0][1].shape[0], cols[0].shape[1]
    args, layout, aliases = [], [], {}
    for at, (pack, strength, addends) in enumerate(row_packs):
        layout.append((len(pack), tuple(len(addend) for addend in addends)))
        args += [*pack, strength]
        if addends and len(addends[0]) == pieces and dtype == addends[0][0].dtype:
            aliases.update({len(args) + i: at * pieces + i for i in range(pieces)})
        args += sum(addends, [])
    return call(
        functools.partial(window_kernel, tuple(layout), pieces, len(cols)),
        [((size // pieces, width), dtype)] * (pieces * len(row_packs)),
        (*args, *cols),
        "window",
        aliases=aliases,
        flops=weight * len(row_packs) * size**2 * width,
    )


def finish_kernel(here_ref, *refs):
    pieces, (away_ref, out_ref) = refs[:-2], refs[-2:]
    rows = here_ref.shape[0] // len(pieces)
    for i, piece_ref in enumerate(pieces):
        part = slice(i * rows, (i + 1) * rows)
        total = here_ref[part, :] + piece_ref[...].astype(jnp.float32) + away_ref[part, :].astype(jnp.float32)
        out_ref[part, :] = total * (1.0 / TEMPER)


def per_device(views, log_sum_exp, loss_weight, partner):
    dp_place, sub_place = lax.axis_index("dp"), lax.axis_index("sub")
    loop_size = lax.axis_size("dp")
    chips = loop_size // 2
    size = views.shape[0]

    onward = []
    for place in range(chips):
        turn = 1 if (place + 1) % (chips // GROUPS) == 0 else 0
        later = (place + 1) % chips
        for sub in range(2):
            onward.append(((2 * place) * 2 + sub, (2 * later) * 2 + (sub ^ turn)))
            onward.append(((2 * later + 1) * 2 + (sub ^ turn), (2 * place + 1) * 2 + sub))
    cores = [(place, place ^ 1) for place in range(loop_size)]

    def chip_next(value):
        return lax.ppermute(value, ("dp", "sub"), onward)

    def core_swap(value):
        return lax.ppermute(value, "dp", cores)

    def sub_swap(value):
        return lax.ppermute(value, "sub", [(0, 1), (1, 0)])

    place = ((dp_place % 2) * 2 + sub_place).astype(jnp.int32).reshape(1)
    whole, *own = pack_views(place, views, log_sum_exp, loss_weight, partner)
    core = [core_swap(own[0])]
    for chunk in own[1:]:
        core.append(core_swap(hold(chunk, core[-1])))
    strengths, totals, columns = {}, {"core": [], "far": []}, {}
    strengths["own"], token = block_terms(True, [whole], whole, core)
    totals["own"] = [[token]]
    coming = {"core": [chip_next(chunk) for chunk in core], "own": [chip_next(hold(whole, token))]}
    other = [sub_swap(chunk) for chunk in own]

    reach = STEPS // 2
    legs = [(kind, step) for step in range(1, reach) for kind in ("core", "own")] + [("core", reach)]
    packs = {"own": [whole], "core": core}
    strengths["core"] = strengths_of(core, size)

    def run(plan, token, arrived):
        for name, rows in plan:
            group = [
                (packs[r], strengths[r], [[hold(hold(a, arrived), token) for a in addend] for addend in totals[r]])
                for r in rows
            ]
            if name == f"own{reach - 1}" and rows[0] in ("core", "far"):
                sums = window_terms(group, columns[name], jnp.bfloat16, 2)
                totals[rows[0]] = [sums]
            else:
                sums = window_terms(group, columns[name], weight=16 if arrivals < 9 else 0)
                totals.update({r: [[value]] for r, value in zip(rows, sums, strict=True)})
            token = sums[0]
        return token

    arrivals = 0
    for kind, step in legs:
        arrived, sent = [], []
        columns[f"{kind}{step}"] = arrived
        for pack in coming[kind]:
            pack = hold(pack, token)
            token = hold(token, pack)
            arrived.append(pack)
            if step < reach - (kind == "own"):
                sent.append(chip_next(pack))
            arrivals += 1
            token = run(PLAN.get(arrivals, ()), token, pack)
            if arrivals == ROWS_AT:
                other = [hold(hold(part, pack), token) for part in other]
                strengths["other"], token = block_terms(False, other, whole, core)
                far = [core_swap(part) for part in other]
                packs["other"], packs["far"] = other, far
                totals["other"] = [[token]]
                strengths["far"] = strengths_of(far, size)
        coming[kind] = sent
    back = [core_swap(piece) for piece in totals["far"][0]]
    (away,) = window_terms([(packs["other"], strengths["other"], totals["other"] + [back])], arrived, jnp.bfloat16)
    token = run(BESIDE, away, pack)
    away = sub_swap(away)
    back = [core_swap(piece) for piece in totals["core"][0]]
    (here,) = window_terms([(packs["own"], strengths["own"], totals["own"])], arrived)
    return call(finish_kernel, [(here.shape, jnp.float32)], (here, *back, away), "finish")[0]


def solution(mesh):
    in_specs = (P(("dp", "sub"), None), P(("dp", "sub")), P(("dp", "sub")), P(("dp", "sub")))
    out_specs = P(("dp", "sub"), None)
    return jax.shard_map(per_device, mesh=mesh, in_specs=in_specs, out_specs=out_specs, check_vma=False)
```

```python
import functools
import math

import jax
import jax.numpy as jnp
from jax import lax
from jax.experimental import pallas as pl
from jax.experimental.pallas import tpu as pltpu
from jax.sharding import PartitionSpec as P

STEPS = 8
TEMPER = 0.07
SHIFT = 11.5
SCALE = math.log2(math.e) / TEMPER
OFFSET = SHIFT * math.log2(math.e)
EXTRA = 16
CHUNKS = 2
GROUPS = 2
VMEM = 8 * 2**20
WHOLE = pl.BlockSpec(memory_space=pltpu.VMEM)

PLAN = {
    2: [("core1", ("own", "core"))],
    4: [("own1", ("own", "core"))],
    6: [("core1", ("other",)), ("own1", ("other",))],
    8: [("core1", ("far",)), ("own1", ("far",))],
    9: [("core2", ("other", "far"))],
    10: [("own2", ("other", "far")), ("core3", ("other", "far"))],
    12: [("own3", ("far",)), ("own3", ("other",))],
}
FAR_AT = 8
BESIDE = [(name, ("own", "core")) for name in ("core2", "own2", "core3")] + [("own3", ("core",)), ("own3", ("own",))]
ROWS_AT = 5


def hold(value, token):
    return lax.optimization_barrier((value, token))[0]


def call(kernel, shapes, args, name, aliases=None, flops=0, specs=None):
    return pl.pallas_call(
        kernel,
        out_shape=[jax.ShapeDtypeStruct(shape, dtype) for shape, dtype in shapes],
        in_specs=specs or [WHOLE] * len(args),
        out_specs=[WHOLE] * len(shapes),
        input_output_aliases=aliases or {},
        compiler_params=pltpu.CompilerParams(vmem_limit_bytes=VMEM),
        cost_estimate=pl.CostEstimate(flops=flops, bytes_accessed=0, transcendentals=0),
        name=name,
    )(*args)


def split3(value):
    high = value.astype(jnp.bfloat16)
    rest = value - high.astype(jnp.float32)
    mid = rest.astype(jnp.bfloat16)
    low = (rest - mid.astype(jnp.float32)).astype(jnp.bfloat16)
    return [high.astype(jnp.float32), mid.astype(jnp.float32), low.astype(jnp.float32)]


def pack_kernel(place_ref, views_ref, lse_ref, weight_ref, partner_ref, whole_ref, *chunk_refs):
    total = views_ref.shape[0]
    rows = total // CHUNKS
    weight = weight_ref[...]
    strength = weight * jnp.exp(SHIFT - lse_ref[...])
    local = partner_ref[...] & 2047
    place = jnp.full(weight.shape, place_ref[0] * total, jnp.int32).astype(jnp.float32)
    lines = split3(strength) + split3(weight)
    lines += [(local >> 8).astype(jnp.float32), (local & 255).astype(jnp.float32), place]
    lines += [jnp.zeros_like(weight)] * (EXTRA - len(lines))
    extra = jnp.concatenate(lines, axis=0).astype(jnp.bfloat16)
    chunk_refs[0][rows:, :] = extra
    whole_ref[total:, :] = extra
    for i, chunk_ref in enumerate(chunk_refs):
        chunk = views_ref[i * rows : (i + 1) * rows, :].astype(jnp.bfloat16)
        chunk_ref[:rows, :] = chunk
        whole_ref[i * rows : (i + 1) * rows, :] = chunk


def pack_views(place, views, lse, weight, partner):
    rows, width = views.shape
    sizes = [rows + EXTRA] + [rows // CHUNKS + (EXTRA if i == 0 else 0) for i in range(CHUNKS)]
    line = (1, rows)
    return call(
        pack_kernel,
        [((size, width), jnp.bfloat16) for size in sizes],
        (place, views, lse.reshape(line), weight.reshape(line), partner.reshape(line)),
        "pack",
        specs=[pl.BlockSpec(memory_space=pltpu.SMEM)] + [WHOLE] * 4,
    )


def statistics(first_ref):
    rows = first_ref.shape[0] - EXTRA
    lines = first_ref[rows:, :].astype(jnp.float32)
    strength = lines[0:1] + lines[1:2] + lines[2:3]
    weight = lines[3:4] + lines[4:5] + lines[5:6]
    partner = lines[6:7] * 256.0 + lines[7:8]
    return strength, weight, partner, lines[8:9]


def part_of(ref, offset):
    return ref if offset is None else ref.at[pl.ds(offset, ref.shape[0] // 2)]


def joined(chunk_refs):
    first = chunk_refs[0][: chunk_refs[0].shape[0] - EXTRA, :]
    rest = [ref[...] for ref in chunk_refs[1:]]
    return jnp.concatenate([first] + rest, axis=0) if rest else first


def spread(line):
    return jnp.broadcast_to(line, (128, line.shape[1])).T


def wide(column, width):
    return jnp.concatenate([column] * (width // 128), axis=1)


def scores_of(rows, cols):
    return lax.dot_general(rows, cols, (((1,), (1,)), ((), ())), preferred_element_type=jnp.float32)


def block_kernel(diagonal, row_ref, own_ref, *refs):
    core_refs, (strength_ref, total_ref, *both) = refs[:CHUNKS], refs[CHUNKS:]
    row_refs = [row_ref]
    size = total_ref.shape[0]
    row_strength, row_weight, _, row_place = statistics(row_refs[0])
    row_strength, row_weight = spread(row_strength), spread(row_weight)
    strength_ref[...] = row_strength
    rows = joined(row_refs)
    row_at = lax.broadcasted_iota(jnp.int32, (size, size), 0)
    total = None
    for col_refs in ([own_ref], core_refs):
        strength, weight, partner, _ = statistics(col_refs[0])
        cols = joined(col_refs)
        raised = jnp.exp2(scores_of(rows, cols) * SCALE - OFFSET)
        value = raised * (wide(row_strength, size) + strength)
        pair = partner == row_at.astype(jnp.float32) + row_place
        value = value - jnp.where(pair, wide(row_weight, size) + weight, 0.0)
        if diagonal and total is None:
            col_at = lax.broadcasted_iota(jnp.int32, (size, size), 1)
            value = jnp.where(row_at == col_at, 0.0, value)
        term = jnp.dot(value.astype(jnp.bfloat16), cols, preferred_element_type=jnp.float32)
        total = term if total is None else total + term
    total_ref[...] = total
    if both:
        both[0][:size, :] = joined(core_refs)
        both[0][size:, :] = core_refs[0][core_refs[0].shape[0] - EXTRA :, :]


def block_terms(diagonal, rows, own, core):
    size, width = own.shape[0] - EXTRA, own.shape[1]
    both = [(own.shape, jnp.bfloat16)] if diagonal else []
    return call(
        functools.partial(block_kernel, diagonal),
        [((size, 128), jnp.float32), ((size, width), jnp.float32)] + both,
        (rows, own, *core),
        "own_rows" if diagonal else "other_rows",
        flops=32 * size**2 * width,
    )


def spread_kernel(offset, first_ref, out_ref):
    out_ref[...] = spread(statistics(part_of(first_ref, offset))[0])


def strengths_of(pack, size):
    array, offset = pack[0]
    kernel = functools.partial(spread_kernel, offset)
    return call(kernel, [((size, 128), jnp.float32)], (array,), "spread")[0]


def window_kernel(layout, pieces, count, *refs):
    refs = list(refs)
    parts = []
    for offsets, addends in layout:
        pack, strength = [part_of(refs.pop(0), offset) for offset in offsets], refs.pop(0)
        parts.append((pack, strength, [[refs.pop(0) for _ in range(count)] for count in addends]))
    cols_refs = [refs.pop(0) for _ in range(count)]
    strength, _, _, _ = statistics(cols_refs[0])
    cols = joined(cols_refs)
    for at, (pack, row_strength, addends) in enumerate(parts):
        size = row_strength.shape[0]
        raised = jnp.exp2(scores_of(joined(pack), cols) * SCALE - OFFSET)
        value = (raised * (wide(row_strength[...], size) + strength)).astype(jnp.bfloat16)
        total = jnp.dot(value, cols, preferred_element_type=jnp.float32)
        for addend in addends:
            whole = [ref[...].astype(jnp.float32) for ref in addend]
            total = total + (jnp.concatenate(whole, axis=0) if len(whole) > 1 else whole[0])
        for i, out_ref in enumerate(refs[at * pieces : (at + 1) * pieces]):
            rows = out_ref.shape[0]
            out_ref[...] = total[i * rows : (i + 1) * rows, :].astype(out_ref.dtype)


def window_terms(row_packs, cols, dtype=jnp.float32, pieces=1, weight=0):
    size, width = row_packs[0][1].shape[0], cols[0].shape[1]
    args, layout, aliases = [], [], {}
    for at, (pack, strength, addends) in enumerate(row_packs):
        layout.append((tuple(offset for _, offset in pack), tuple(len(addend) for addend in addends)))
        args += [*[array for array, _ in pack], strength]
        if addends and len(addends[0]) == pieces and dtype == addends[0][0].dtype:
            aliases.update({len(args) + i: at * pieces + i for i in range(pieces)})
        args += sum(addends, [])
    return call(
        functools.partial(window_kernel, tuple(layout), pieces, len(cols)),
        [((size // pieces, width), dtype)] * (pieces * len(row_packs)),
        (*args, *cols),
        "window",
        aliases=aliases,
        flops=weight * len(row_packs) * size**2 * width,
    )


def finish_kernel(here_ref, *refs):
    pieces, (away_ref, out_ref) = refs[:-2], refs[-2:]
    rows = here_ref.shape[0] // len(pieces)
    for i, piece_ref in enumerate(pieces):
        part = slice(i * rows, (i + 1) * rows)
        total = here_ref[part, :] + piece_ref[...].astype(jnp.float32) + away_ref[part, :].astype(jnp.float32)
        out_ref[part, :] = total * (1.0 / TEMPER)


def per_device(views, log_sum_exp, loss_weight, partner):
    dp_place, sub_place = lax.axis_index("dp"), lax.axis_index("sub")
    loop_size = lax.axis_size("dp")
    chips = loop_size // 2
    size = views.shape[0]

    onward = []
    for place in range(chips):
        turn = 1 if (place + 1) % (chips // GROUPS) == 0 else 0
        later = (place + 1) % chips
        for sub in range(2):
            onward.append(((2 * place) * 2 + sub, (2 * later) * 2 + (sub ^ turn)))
            onward.append(((2 * later + 1) * 2 + (sub ^ turn), (2 * place + 1) * 2 + sub))
    cores = [(place, place ^ 1) for place in range(loop_size)]

    def chip_next(value):
        return lax.ppermute(value, ("dp", "sub"), onward)

    def core_swap(value):
        return lax.ppermute(value, "dp", cores)

    def sub_swap(value):
        return lax.ppermute(value, "sub", [(0, 1), (1, 0)])

    place = ((dp_place % 2) * 2 + sub_place).astype(jnp.int32).reshape(1)
    whole, *own = pack_views(place, views, log_sum_exp, loss_weight, partner)
    core = [core_swap(own[0])]
    for chunk in own[1:]:
        core.append(core_swap(hold(chunk, core[-1])))
    strengths, totals, columns = {}, {"core": [], "far": []}, {}
    strengths["own"], token, core_whole = block_terms(True, whole, whole, core)
    totals["own"] = [[token]]
    coming = {"core": [chip_next(chunk) for chunk in core], "own": [chip_next(hold(chunk, token)) for chunk in own]}
    other = sub_swap(whole)
    far = sub_swap(hold(core_whole, other))

    reach = STEPS // 2
    legs = [(kind, step) for step in range(1, reach) for kind in ("core", "own")] + [("core", reach)]
    packs = {"own": [(whole, None)], "core": [(chunk, None) for chunk in core]}
    strengths["core"] = strengths_of(packs["core"], size)

    def run(plan, token, arrived):
        for name, rows in plan:
            group = [
                (packs[r], strengths[r], [[hold(hold(a, arrived), token) for a in addend] for addend in totals[r]])
                for r in rows
            ]
            if name == f"own{reach - 1}" and rows[0] in ("core", "far"):
                sums = window_terms(group, columns[name], jnp.bfloat16, 2)
                totals[rows[0]] = [sums]
            else:
                sums = window_terms(group, columns[name], weight=16 if arrivals < 9 else 0)
                totals.update({r: [[value]] for r, value in zip(rows, sums, strict=True)})
            token = sums[0]
        return token

    arrivals = 0
    for kind, step in legs:
        arrived, sent = [], []
        columns[f"{kind}{step}"] = arrived
        for pack in coming[kind]:
            pack = hold(pack, token)
            token = hold(token, pack)
            arrived.append(pack)
            if step < reach - (kind == "own"):
                sent.append(chip_next(pack))
            arrivals += 1
            if arrivals == FAR_AT:
                far = hold(hold(far, pack), token)
                packs["far"] = [(far, None)]
                strengths["far"] = strengths_of(packs["far"], size)
            token = run(PLAN.get(arrivals, ()), token, pack)
            if arrivals == ROWS_AT:
                other = hold(hold(other, pack), token)
                strengths["other"], token = block_terms(False, other, whole, core)
                totals["other"] = [[token]]
                packs["other"] = [(other, None)]
        coming[kind] = sent
    back = [core_swap(piece) for piece in totals["far"][0]]
    (away,) = window_terms([(packs["other"], strengths["other"], totals["other"] + [back])], arrived, jnp.bfloat16)
    token = run(BESIDE, away, pack)
    away = sub_swap(away)
    back = [core_swap(piece) for piece in totals["core"][0]]
    (here,) = window_terms([(packs["own"], strengths["own"], totals["own"])], arrived)
    return call(finish_kernel, [(here.shape, jnp.float32)], (here, *back, away), "finish")[0]


def solution(mesh):
    in_specs = (P(("dp", "sub"), None), P(("dp", "sub")), P(("dp", "sub")), P(("dp", "sub")))
    out_specs = P(("dp", "sub"), None)
    return jax.shard_map(per_device, mesh=mesh, in_specs=in_specs, out_specs=out_specs, check_vma=False)
```

```python
import functools
import math

import jax
import jax.numpy as jnp
from jax import lax
from jax.experimental import pallas as pl
from jax.experimental.pallas import tpu as pltpu
from jax.sharding import PartitionSpec as P

STEPS = 8
TEMPER = 0.07
SHIFT = 11.5
SCALE = math.log2(math.e) / TEMPER
OFFSET = SHIFT * math.log2(math.e)
EXTRA = 16
CHUNKS = 2
GROUPS = 2
VMEM = 8 * 2**20
WHOLE = pl.BlockSpec(memory_space=pltpu.VMEM)

PLAN = {
    2: [("core1", ("own", "core"))],
    4: [("own1", ("own", "core"))],
    6: [("core1", ("other",)), ("own1", ("other",)), ("core2", ("other",))],
    8: [("core1", ("far",)), ("own1", ("far",)), ("core2", ("far",))],
    9: [("own2", ("other", "far"))],
    10: [("core3", ("other", "far"))],
    12: [("own3", ("far",)), ("own3", ("other",))],
}
FAR_AT = 8
BESIDE = [(name, ("own", "core")) for name in ("core2", "own2", "core3")] + [("own3", ("core",)), ("own3", ("own",))]
ROWS_AT = 5


def hold(value, token):
    return lax.optimization_barrier((value, token))[0]


def call(kernel, shapes, args, name, aliases=None, flops=0, specs=None):
    return pl.pallas_call(
        kernel,
        out_shape=[jax.ShapeDtypeStruct(shape, dtype) for shape, dtype in shapes],
        in_specs=specs or [WHOLE] * len(args),
        out_specs=[WHOLE] * len(shapes),
        input_output_aliases=aliases or {},
        compiler_params=pltpu.CompilerParams(vmem_limit_bytes=VMEM),
        cost_estimate=pl.CostEstimate(flops=flops, bytes_accessed=0, transcendentals=0),
        name=name,
    )(*args)


def split3(value):
    high = value.astype(jnp.bfloat16)
    rest = value - high.astype(jnp.float32)
    mid = rest.astype(jnp.bfloat16)
    low = (rest - mid.astype(jnp.float32)).astype(jnp.bfloat16)
    return [high.astype(jnp.float32), mid.astype(jnp.float32), low.astype(jnp.float32)]


def pack_kernel(place_ref, views_ref, lse_ref, weight_ref, partner_ref, whole_ref, *chunk_refs):
    total = views_ref.shape[0]
    rows = total // CHUNKS
    weight = weight_ref[...]
    strength = weight * jnp.exp(SHIFT - lse_ref[...])
    local = partner_ref[...] & 2047
    place = jnp.full(weight.shape, place_ref[0] * total, jnp.int32).astype(jnp.float32)
    lines = split3(strength) + split3(weight)
    lines += [(local >> 8).astype(jnp.float32), (local & 255).astype(jnp.float32), place]
    lines += [jnp.zeros_like(weight)] * (EXTRA - len(lines))
    extra = jnp.concatenate(lines, axis=0).astype(jnp.bfloat16)
    chunk_refs[0][rows:, :] = extra
    whole_ref[total:, :] = extra
    for i, chunk_ref in enumerate(chunk_refs):
        chunk = views_ref[i * rows : (i + 1) * rows, :].astype(jnp.bfloat16)
        chunk_ref[:rows, :] = chunk
        whole_ref[i * rows : (i + 1) * rows, :] = chunk


def pack_views(place, views, lse, weight, partner):
    rows, width = views.shape
    sizes = [rows + EXTRA] + [rows // CHUNKS + (EXTRA if i == 0 else 0) for i in range(CHUNKS)]
    line = (1, rows)
    return call(
        pack_kernel,
        [((size, width), jnp.bfloat16) for size in sizes],
        (place, views, lse.reshape(line), weight.reshape(line), partner.reshape(line)),
        "pack",
        specs=[pl.BlockSpec(memory_space=pltpu.SMEM)] + [WHOLE] * 4,
    )


def statistics(first_ref):
    rows = first_ref.shape[0] - EXTRA
    lines = first_ref[rows:, :].astype(jnp.float32)
    strength = lines[0:1] + lines[1:2] + lines[2:3]
    weight = lines[3:4] + lines[4:5] + lines[5:6]
    partner = lines[6:7] * 256.0 + lines[7:8]
    return strength, weight, partner, lines[8:9]


def part_of(ref, offset):
    return ref if offset is None else ref.at[pl.ds(offset, ref.shape[0] // 2)]


def joined(chunk_refs):
    first = chunk_refs[0][: chunk_refs[0].shape[0] - EXTRA, :]
    rest = [ref[...] for ref in chunk_refs[1:]]
    return jnp.concatenate([first] + rest, axis=0) if rest else first


def spread(line):
    return jnp.broadcast_to(line, (128, line.shape[1])).T


def wide(column, width):
    return jnp.concatenate([column] * (width // 128), axis=1)


def scores_of(rows, cols):
    return lax.dot_general(rows, cols, (((1,), (1,)), ((), ())), preferred_element_type=jnp.float32)


def block_kernel(diagonal, row_ref, own_ref, *refs):
    core_refs, (strength_ref, total_ref, *both) = refs[:CHUNKS], refs[CHUNKS:]
    row_refs = [row_ref]
    size = total_ref.shape[0]
    row_strength, row_weight, _, row_place = statistics(row_refs[0])
    row_strength, row_weight = spread(row_strength), spread(row_weight)
    strength_ref[...] = row_strength
    rows = joined(row_refs)
    row_at = lax.broadcasted_iota(jnp.int32, (size, size), 0)
    total = None
    for col_refs in ([own_ref], core_refs):
        strength, weight, partner, _ = statistics(col_refs[0])
        cols = joined(col_refs)
        raised = jnp.exp2(scores_of(rows, cols) * SCALE - OFFSET)
        value = raised * (wide(row_strength, size) + strength)
        pair = partner == row_at.astype(jnp.float32) + row_place
        value = value - jnp.where(pair, wide(row_weight, size) + weight, 0.0)
        if diagonal and total is None:
            col_at = lax.broadcasted_iota(jnp.int32, (size, size), 1)
            value = jnp.where(row_at == col_at, 0.0, value)
        term = jnp.dot(value.astype(jnp.bfloat16), cols, preferred_element_type=jnp.float32)
        total = term if total is None else total + term
    total_ref[...] = total
    if both:
        both[0][:size, :] = joined(core_refs)
        both[0][size:, :] = core_refs[0][core_refs[0].shape[0] - EXTRA :, :]


def block_terms(diagonal, rows, own, core):
    size, width = own.shape[0] - EXTRA, own.shape[1]
    both = [(own.shape, jnp.bfloat16)] if diagonal else []
    return call(
        functools.partial(block_kernel, diagonal),
        [((size, 128), jnp.float32), ((size, width), jnp.float32)] + both,
        (rows, own, *core),
        "own_rows" if diagonal else "other_rows",
        flops=32 * size**2 * width,
    )


def spread_kernel(offset, first_ref, out_ref):
    out_ref[...] = spread(statistics(part_of(first_ref, offset))[0])


def strengths_of(pack, size):
    array, offset = pack[0]
    kernel = functools.partial(spread_kernel, offset)
    return call(kernel, [((size, 128), jnp.float32)], (array,), "spread")[0]


def window_kernel(layout, pieces, count, *refs):
    refs = list(refs)
    parts = []
    for offsets, addends in layout:
        pack, strength = [part_of(refs.pop(0), offset) for offset in offsets], refs.pop(0)
        parts.append((pack, strength, [[refs.pop(0) for _ in range(count)] for count in addends]))
    cols_refs = [refs.pop(0) for _ in range(count)]
    strength, _, _, _ = statistics(cols_refs[0])
    cols = joined(cols_refs)
    for at, (pack, row_strength, addends) in enumerate(parts):
        size = row_strength.shape[0]
        raised = jnp.exp2(scores_of(joined(pack), cols) * SCALE - OFFSET)
        value = (raised * (wide(row_strength[...], size) + strength)).astype(jnp.bfloat16)
        total = jnp.dot(value, cols, preferred_element_type=jnp.float32)
        for addend in addends:
            whole = [ref[...].astype(jnp.float32) for ref in addend]
            total = total + (jnp.concatenate(whole, axis=0) if len(whole) > 1 else whole[0])
        for i, out_ref in enumerate(refs[at * pieces : (at + 1) * pieces]):
            rows = out_ref.shape[0]
            out_ref[...] = total[i * rows : (i + 1) * rows, :].astype(out_ref.dtype)


def window_terms(row_packs, cols, dtype=jnp.float32, pieces=1, weight=0):
    size, width = row_packs[0][1].shape[0], cols[0].shape[1]
    args, layout, aliases = [], [], {}
    for at, (pack, strength, addends) in enumerate(row_packs):
        layout.append((tuple(offset for _, offset in pack), tuple(len(addend) for addend in addends)))
        args += [*[array for array, _ in pack], strength]
        if addends and len(addends[0]) == pieces and dtype == addends[0][0].dtype:
            aliases.update({len(args) + i: at * pieces + i for i in range(pieces)})
        args += sum(addends, [])
    return call(
        functools.partial(window_kernel, tuple(layout), pieces, len(cols)),
        [((size // pieces, width), dtype)] * (pieces * len(row_packs)),
        (*args, *cols),
        "window",
        aliases=aliases,
        flops=weight * len(row_packs) * size**2 * width,
    )


def finish_kernel(here_ref, *refs):
    pieces, (away_ref, out_ref) = refs[:-2], refs[-2:]
    rows = here_ref.shape[0] // len(pieces)
    for i, piece_ref in enumerate(pieces):
        part = slice(i * rows, (i + 1) * rows)
        total = here_ref[part, :] + piece_ref[...].astype(jnp.float32) + away_ref[part, :].astype(jnp.float32)
        out_ref[part, :] = total * (1.0 / TEMPER)


def per_device(views, log_sum_exp, loss_weight, partner):
    dp_place, sub_place = lax.axis_index("dp"), lax.axis_index("sub")
    loop_size = lax.axis_size("dp")
    chips = loop_size // 2
    size = views.shape[0]

    onward = []
    for place in range(chips):
        turn = 1 if (place + 1) % (chips // GROUPS) == 0 else 0
        later = (place + 1) % chips
        for sub in range(2):
            onward.append(((2 * place) * 2 + sub, (2 * later) * 2 + (sub ^ turn)))
            onward.append(((2 * later + 1) * 2 + (sub ^ turn), (2 * place + 1) * 2 + sub))
    cores = [(place, place ^ 1) for place in range(loop_size)]

    def chip_next(value):
        return lax.ppermute(value, ("dp", "sub"), onward)

    def core_swap(value):
        return lax.ppermute(value, "dp", cores)

    def sub_swap(value):
        return lax.ppermute(value, "sub", [(0, 1), (1, 0)])

    place = ((dp_place % 2) * 2 + sub_place).astype(jnp.int32).reshape(1)
    whole, *own = pack_views(place, views, log_sum_exp, loss_weight, partner)
    core = [core_swap(own[0])]
    for chunk in own[1:]:
        core.append(core_swap(hold(chunk, core[-1])))
    strengths, totals, columns = {}, {"core": [], "far": []}, {}
    strengths["own"], token, core_whole = block_terms(True, whole, whole, core)
    totals["own"] = [[token]]
    coming = {"core": [chip_next(chunk) for chunk in core], "own": [chip_next(hold(chunk, token)) for chunk in own]}
    other = sub_swap(whole)
    far = sub_swap(hold(core_whole, other))

    reach = STEPS // 2
    legs = [(kind, step) for step in range(1, reach) for kind in ("core", "own")] + [("core", reach)]
    packs = {"own": [(whole, None)], "core": [(chunk, None) for chunk in core]}
    strengths["core"] = strengths_of(packs["core"], size)

    def run(plan, token, arrived):
        for name, rows in plan:
            group = [
                (packs[r], strengths[r], [[hold(hold(a, arrived), token) for a in addend] for addend in totals[r]])
                for r in rows
            ]
            if name == f"own{reach - 1}" and rows[0] in ("core", "far"):
                sums = window_terms(group, columns[name], jnp.bfloat16, 2)
                totals[rows[0]] = [sums]
            else:
                sums = window_terms(group, columns[name], weight=8 if arrivals < 10 else 0)
                totals.update({r: [[value]] for r, value in zip(rows, sums, strict=True)})
            token = sums[0]
        return token

    arrivals = 0
    for kind, step in legs:
        arrived, sent = [], []
        columns[f"{kind}{step}"] = arrived
        for pack in coming[kind]:
            pack = hold(pack, token)
            token = hold(token, pack)
            arrived.append(pack)
            if step < reach - (kind == "own"):
                sent.append(chip_next(pack))
            arrivals += 1
            if arrivals == FAR_AT:
                far = hold(hold(far, pack), token)
                packs["far"] = [(far, None)]
                strengths["far"] = strengths_of(packs["far"], size)
            token = run(PLAN.get(arrivals, ()), token, pack)
            if arrivals == ROWS_AT:
                other = hold(hold(other, pack), token)
                strengths["other"], token = block_terms(False, other, whole, core)
                totals["other"] = [[token]]
                packs["other"] = [(other, None)]
        coming[kind] = sent
    back = [core_swap(piece) for piece in totals["far"][0]]
    (away,) = window_terms([(packs["other"], strengths["other"], totals["other"] + [back])], arrived, jnp.bfloat16)
    token = run(BESIDE, away, pack)
    away = sub_swap(away)
    back = [core_swap(piece) for piece in totals["core"][0]]
    (here,) = window_terms([(packs["own"], strengths["own"], totals["own"])], arrived)
    return call(finish_kernel, [(here.shape, jnp.float32)], (here, *back, away), "finish")[0]


def solution(mesh):
    in_specs = (P(("dp", "sub"), None), P(("dp", "sub")), P(("dp", "sub")), P(("dp", "sub")))
    out_specs = P(("dp", "sub"), None)
    return jax.shard_map(per_device, mesh=mesh, in_specs=in_specs, out_specs=out_specs, check_vma=False)
```

```python
import functools
import math

import jax
import jax.numpy as jnp
from jax import lax
from jax.experimental import pallas as pl
from jax.experimental.pallas import tpu as pltpu
from jax.sharding import PartitionSpec as P

STEPS = 8
TEMPER = 0.07
SHIFT = 11.5
SCALE = math.log2(math.e) / TEMPER
OFFSET = SHIFT * math.log2(math.e)
EXTRA = 16
CHUNKS = 2
GROUPS = 2
VMEM = 8 * 2**20
WHOLE = pl.BlockSpec(memory_space=pltpu.VMEM)

PLAN = {
    2: [("core1", ("own", "core"))],
    4: [("own1", ("own", "core"))],
    6: [("core1", ("other",)), ("own1", ("other",)), ("core2", ("other",))],
    8: [("core1", ("far",)), ("own1", ("far",)), ("core2", ("far",))],
    9: [("own2", ("other", "far"))],
    10: [("core3", ("other", "far"))],
    12: [("own3", ("far",)), ("own3", ("other",))],
}
FAR_AT = 8
BESIDE = [(name, ("own", "core")) for name in ("core2", "own2", "core3")] + [("own3", ("core",)), ("own3", ("own",))]
ROWS_AT = 5


def hold(value, token):
    return lax.optimization_barrier((value, token))[0]


def call(kernel, shapes, args, name, aliases=None, flops=0, specs=None):
    return pl.pallas_call(
        kernel,
        out_shape=[jax.ShapeDtypeStruct(shape, dtype) for shape, dtype in shapes],
        in_specs=specs or [WHOLE] * len(args),
        out_specs=[WHOLE] * len(shapes),
        input_output_aliases=aliases or {},
        compiler_params=pltpu.CompilerParams(vmem_limit_bytes=VMEM),
        cost_estimate=pl.CostEstimate(flops=flops, bytes_accessed=0, transcendentals=0),
        name=name,
    )(*args)


def split3(value):
    high = value.astype(jnp.bfloat16)
    rest = value - high.astype(jnp.float32)
    mid = rest.astype(jnp.bfloat16)
    low = (rest - mid.astype(jnp.float32)).astype(jnp.bfloat16)
    return [high.astype(jnp.float32), mid.astype(jnp.float32), low.astype(jnp.float32)]


def pack_kernel(place_ref, views_ref, lse_ref, weight_ref, partner_ref, whole_ref, *chunk_refs):
    total = views_ref.shape[0]
    rows = total // CHUNKS
    weight = weight_ref[...]
    strength = weight * jnp.exp(SHIFT - lse_ref[...])
    local = partner_ref[...] & 2047
    place = jnp.full(weight.shape, place_ref[0] * total, jnp.int32).astype(jnp.float32)
    lines = split3(strength) + split3(weight)
    lines += [(local >> 8).astype(jnp.float32), (local & 255).astype(jnp.float32), place]
    lines += [jnp.zeros_like(weight)] * (EXTRA - len(lines))
    extra = jnp.concatenate(lines, axis=0).astype(jnp.bfloat16)
    chunk_refs[0][rows:, :] = extra
    whole_ref[total:, :] = extra
    for i, chunk_ref in enumerate(chunk_refs):
        chunk = views_ref[i * rows : (i + 1) * rows, :].astype(jnp.bfloat16)
        chunk_ref[:rows, :] = chunk
        whole_ref[i * rows : (i + 1) * rows, :] = chunk


def pack_views(place, views, lse, weight, partner):
    rows, width = views.shape
    sizes = [rows + EXTRA] + [rows // CHUNKS + (EXTRA if i == 0 else 0) for i in range(CHUNKS)]
    line = (1, rows)
    return call(
        pack_kernel,
        [((size, width), jnp.bfloat16) for size in sizes],
        (place, views, lse.reshape(line), weight.reshape(line), partner.reshape(line)),
        "pack",
        specs=[pl.BlockSpec(memory_space=pltpu.SMEM)] + [WHOLE] * 4,
    )


def statistics(first_ref):
    rows = first_ref.shape[0] - EXTRA
    lines = first_ref[rows:, :].astype(jnp.float32)
    strength = lines[0:1] + lines[1:2] + lines[2:3]
    weight = lines[3:4] + lines[4:5] + lines[5:6]
    partner = lines[6:7] * 256.0 + lines[7:8]
    return strength, weight, partner, lines[8:9]


def part_of(ref, offset):
    return ref if offset is None else ref.at[pl.ds(offset, ref.shape[0] // 2)]


def joined(chunk_refs):
    first = chunk_refs[0][: chunk_refs[0].shape[0] - EXTRA, :]
    rest = [ref[...] for ref in chunk_refs[1:]]
    return jnp.concatenate([first] + rest, axis=0) if rest else first


def spread(line):
    return jnp.broadcast_to(line, (128, line.shape[1])).T


def wide(column, width):
    return jnp.concatenate([column] * (width // 128), axis=1)


def scores_of(rows, cols):
    return lax.dot_general(rows, cols, (((1,), (1,)), ((), ())), preferred_element_type=jnp.float32)


def block_kernel(diagonal, row_ref, own_ref, *refs):
    core_refs, (strength_ref, total_ref, *both) = refs[:CHUNKS], refs[CHUNKS:]
    row_refs = [row_ref]
    size = total_ref.shape[0]
    row_strength, row_weight, _, row_place = statistics(row_refs[0])
    row_strength, row_weight = spread(row_strength), spread(row_weight)
    strength_ref[...] = row_strength
    rows = joined(row_refs)
    row_at = lax.broadcasted_iota(jnp.int32, (size, size), 0)
    total = None
    for col_refs in ([own_ref], core_refs):
        strength, weight, partner, _ = statistics(col_refs[0])
        cols = joined(col_refs)
        raised = jnp.exp2(scores_of(rows, cols) * SCALE - OFFSET)
        value = raised * (wide(row_strength, size) + strength)
        pair = partner == row_at.astype(jnp.float32) + row_place
        value = value - jnp.where(pair, wide(row_weight, size) + weight, 0.0)
        if diagonal and total is None:
            col_at = lax.broadcasted_iota(jnp.int32, (size, size), 1)
            value = jnp.where(row_at == col_at, 0.0, value)
        term = jnp.dot(value.astype(jnp.bfloat16), cols, preferred_element_type=jnp.float32)
        total = term if total is None else total + term
    total_ref[...] = total
    if both:
        both[0][:size, :] = joined(core_refs)
        both[0][size:, :] = core_refs[0][core_refs[0].shape[0] - EXTRA :, :]


def block_terms(diagonal, rows, own, core):
    size, width = own.shape[0] - EXTRA, own.shape[1]
    both = [(own.shape, jnp.bfloat16)] if diagonal else []
    return call(
        functools.partial(block_kernel, diagonal),
        [((size, 128), jnp.float32), ((size, width), jnp.float32)] + both,
        (rows, own, *core),
        "own_rows" if diagonal else "other_rows",
        flops=32 * size**2 * width,
    )


def spread_kernel(offset, first_ref, out_ref):
    out_ref[...] = spread(statistics(part_of(first_ref, offset))[0])


def strengths_of(pack, size):
    array, offset = pack[0]
    kernel = functools.partial(spread_kernel, offset)
    return call(kernel, [((size, 128), jnp.float32)], (array,), "spread")[0]


def window_kernel(layout, pieces, count, *refs):
    refs = list(refs)
    parts = []
    for offsets, addends in layout:
        pack, strength = [part_of(refs.pop(0), offset) for offset in offsets], refs.pop(0)
        parts.append((pack, strength, [[refs.pop(0) for _ in range(count)] for count in addends]))
    cols_refs = [refs.pop(0) for _ in range(count)]
    strength, _, _, _ = statistics(cols_refs[0])
    cols = joined(cols_refs)
    for at, (pack, row_strength, addends) in enumerate(parts):
        size = row_strength.shape[0]
        raised = jnp.exp2(scores_of(joined(pack), cols) * SCALE - OFFSET)
        value = (raised * (wide(row_strength[...], size) + strength)).astype(jnp.bfloat16)
        total = jnp.dot(value, cols, preferred_element_type=jnp.float32)
        for addend in addends:
            whole = [ref[...].astype(jnp.float32) for ref in addend]
            total = total + (jnp.concatenate(whole, axis=0) if len(whole) > 1 else whole[0])
        for i, out_ref in enumerate(refs[at * pieces : (at + 1) * pieces]):
            rows = out_ref.shape[0]
            out_ref[...] = total[i * rows : (i + 1) * rows, :].astype(out_ref.dtype)


def window_terms(row_packs, cols, dtype=jnp.float32, pieces=1, weight=0):
    size, width = row_packs[0][1].shape[0], cols[0].shape[1]
    args, layout, aliases = [], [], {}
    for at, (pack, strength, addends) in enumerate(row_packs):
        layout.append((tuple(offset for _, offset in pack), tuple(len(addend) for addend in addends)))
        args += [*[array for array, _ in pack], strength]
        if addends and len(addends[0]) == pieces and dtype == addends[0][0].dtype:
            aliases.update({len(args) + i: at * pieces + i for i in range(pieces)})
        args += sum(addends, [])
    return call(
        functools.partial(window_kernel, tuple(layout), pieces, len(cols)),
        [((size // pieces, width), dtype)] * (pieces * len(row_packs)),
        (*args, *cols),
        "window",
        aliases=aliases,
        flops=weight * len(row_packs) * size**2 * width,
    )


def finish_kernel(here_ref, *refs):
    pieces, (away_ref, out_ref) = refs[:-2], refs[-2:]
    rows = here_ref.shape[0] // len(pieces)
    for i, piece_ref in enumerate(pieces):
        part = slice(i * rows, (i + 1) * rows)
        total = here_ref[part, :] + piece_ref[...].astype(jnp.float32) + away_ref[part, :].astype(jnp.float32)
        out_ref[part, :] = total * (1.0 / TEMPER)


def per_device(views, log_sum_exp, loss_weight, partner):
    dp_place, sub_place = lax.axis_index("dp"), lax.axis_index("sub")
    loop_size = lax.axis_size("dp")
    chips = loop_size // 2
    size = views.shape[0]

    onward = []
    for place in range(chips):
        turn = 1 if (place + 1) % (chips // GROUPS) == 0 else 0
        later = (place + 1) % chips
        for sub in range(2):
            onward.append(((2 * place) * 2 + sub, (2 * later) * 2 + (sub ^ turn)))
            onward.append(((2 * later + 1) * 2 + (sub ^ turn), (2 * place + 1) * 2 + sub))
    cores = [(place, place ^ 1) for place in range(loop_size)]

    def chip_next(value):
        return lax.ppermute(value, ("dp", "sub"), onward)

    def core_swap(value):
        return lax.ppermute(value, "dp", cores)

    def sub_swap(value):
        return lax.ppermute(value, "sub", [(0, 1), (1, 0)])

    place = ((dp_place % 2) * 2 + sub_place).astype(jnp.int32).reshape(1)
    whole, *own = pack_views(place, views, log_sum_exp, loss_weight, partner)
    core = [core_swap(own[0])]
    for chunk in own[1:]:
        core.append(core_swap(hold(chunk, core[-1])))
    strengths, totals, columns = {}, {"core": [], "far": []}, {}
    strengths["own"], token, core_whole = block_terms(True, whole, whole, core)
    totals["own"] = [[token]]
    coming = {"core": [chip_next(chunk) for chunk in core], "own": [chip_next(hold(chunk, token)) for chunk in own]}
    other = sub_swap(whole)

    reach = STEPS // 2
    legs = [(kind, step) for step in range(1, reach) for kind in ("core", "own")] + [("core", reach)]
    packs = {"own": [(whole, None)], "core": [(chunk, None) for chunk in core]}
    strengths["core"] = strengths_of(packs["core"], size)

    def run(plan, token, arrived):
        for name, rows in plan:
            group = [
                (packs[r], strengths[r], [[hold(hold(a, arrived), token) for a in addend] for addend in totals[r]])
                for r in rows
            ]
            if name == f"own{reach - 1}" and rows[0] in ("core", "far"):
                sums = window_terms(group, columns[name], jnp.bfloat16, 2)
                totals[rows[0]] = [sums]
            else:
                sums = window_terms(group, columns[name], weight=8 if arrivals < 10 else 0)
                totals.update({r: [[value]] for r, value in zip(rows, sums, strict=True)})
            token = sums[0]
        return token

    arrivals = 0
    for kind, step in legs:
        arrived, sent = [], []
        columns[f"{kind}{step}"] = arrived
        for pack in coming[kind]:
            pack = hold(pack, token)
            token = hold(token, pack)
            arrived.append(pack)
            if step < reach - (kind == "own"):
                sent.append(chip_next(pack))
            arrivals += 1
            if arrivals == 2:
                other = hold(other, pack)
                far = sub_swap(hold(core_whole, other))
            if arrivals == FAR_AT:
                far = hold(hold(far, pack), token)
                packs["far"] = [(far, None)]
                strengths["far"] = strengths_of(packs["far"], size)
            token = run(PLAN.get(arrivals, ()), token, pack)
            if arrivals == ROWS_AT:
                other = hold(hold(other, pack), token)
                strengths["other"], token = block_terms(False, other, whole, core)
                totals["other"] = [[token]]
                packs["other"] = [(other, None)]
        coming[kind] = sent
    back = [core_swap(piece) for piece in totals["far"][0]]
    (away,) = window_terms([(packs["other"], strengths["other"], totals["other"] + [back])], arrived, jnp.bfloat16)
    token = run(BESIDE, away, pack)
    away = sub_swap(away)
    back = [core_swap(piece) for piece in totals["core"][0]]
    (here,) = window_terms([(packs["own"], strengths["own"], totals["own"])], arrived)
    return call(finish_kernel, [(here.shape, jnp.float32)], (here, *back, away), "finish")[0]


def solution(mesh):
    in_specs = (P(("dp", "sub"), None), P(("dp", "sub")), P(("dp", "sub")), P(("dp", "sub")))
    out_specs = P(("dp", "sub"), None)
    return jax.shard_map(per_device, mesh=mesh, in_specs=in_specs, out_specs=out_specs, check_vma=False)
```
